256 devices in a mesh: leaf: 128 (over x_lo, z, y, core), sub: 2 (over x_hi).
Axes of the slice: x: 4 (x_hi: 2, x_lo: 2; x = x_hi * 2 + x_lo), y: 4, z: 8, core: 2. Of those that a mesh axis runs over, the one named last changes fastest.
Arguments:
- density: bfloat16 [16, 2097152], P(None, 'leaf'), may hold values from -6 to 6
- coords: float32 [3, 2097152], P(None, 'leaf'), may hold values from 0 to 1
- qweight: float32 [2097152], P('leaf'), may hold values from 0.01 to 0.08
- leaf_basis: bfloat16 [32768, 4096], P('leaf'), may hold values from -0.75 to 0.75
- box_transfer: bfloat16 [32768, 4096], P('leaf'), may hold values from -0.75 to 0.75
- root_transfer: bfloat16 [4096, 4096], P('leaf'), may hold values from -0.75 to 0.75
- box_coupling: bfloat16 [4096, 16, 4096], P(('leaf', 'sub')), may hold values from -1.5 to 1.5
- root_coupling: bfloat16 [128, 12, 4096], P('leaf'), may hold values from -0.75 to 0.75
- near_list: int32 [32768, 12], P(('leaf', 'sub')), may hold values from 0 to 383, as said below
- near_count: int32 [32768], P(('leaf', 'sub')), may hold values from 2 to 12, as said below
- box_list: int32 [4096, 16], P(('leaf', 'sub')), may hold values from 0 to 95, as said below
- root_list: int32 [128, 12], P('leaf'), may hold values from 0 to 127, as said below
- ghost_send: int32 [128, 2, 2, 64], P('leaf', 'sub'), may hold values from 0 to 255
Outputs:
- potential: bfloat16 [16, 2097152], P(None, ('leaf', 'sub'))
The draws below stay inside these ranges and needn't reach their ends.
Inputs may be any that keep to these rules, and one draw needn't show every extreme that they name: `near_list`: in each half of a group every lower and upper ghost slot is named by some live entry, and entry 1 of each leaf names the leaf itself. `near_count`: in each half of a group some leaf has exactly 12 live slots. `box_list`: in each half of a group every box of both neighbouring groups is named by some entry. `root_list`: A row never names its own group, and names no group twice.
All inputs are finite; a program needn't handle non-finite values.
Results may differ from the reference program's by a relative error of at most 0.02.
Values may be sent and summed in bfloat16 or wider, within the bound.
No kernel may reach another device: no remote copies, remote signals or barrier semaphores. Data moves between devices by JAX's collectives and lax.ppermute only.
A program may use at most 128 MiB of HBM per device.

```python
import math
import jax
import jax.numpy as jnp
from jax import lax

LEAF = 64
RANK = 64
RHS = 16
GROUP_LEAVES = 256
NEAR = 12
F1 = 16
F2 = 12
GROUPS = 128
BOX_GROUP = 32
GHOST = 64
LEAVES = 32768
BOXES = 4096
POINTS = 2097152


def draw_near_list(key, part):
    key = jax.random.fold_in(key, 11)
    half_leaves = GROUP_LEAVES // 2
    blocks = LEAVES // half_leaves
    key_rest, key_order = jax.random.split(key, 2)
    random_rows = jax.random.randint(key_rest, (blocks, half_leaves, NEAR), 0, GROUP_LEAVES + 2 * GHOST, dtype=jnp.int32)
    shuffled = jax.vmap(lambda subkey: jax.random.permutation(subkey, half_leaves))(jax.random.split(key_order, blocks)).astype(jnp.int32)
    own_leaf = jnp.arange(blocks, dtype=jnp.int32)[:, None] % 2 * half_leaves + jnp.arange(half_leaves, dtype=jnp.int32)[None, :]
    rows = random_rows.at[:, :, 0].set(GROUP_LEAVES + shuffled).at[:, :, 1].set(own_leaf)
    return rows.reshape(LEAVES, NEAR)


def draw_near_count(key, part):
    key = jax.random.fold_in(key, 12)
    half_leaves = GROUP_LEAVES // 2
    blocks = LEAVES // half_leaves
    key_limit, key_count, key_full = jax.random.split(key, 3)
    limits = jax.random.randint(key_limit, (blocks, 1), 3, NEAR + 1, dtype=jnp.int32)
    drawn = jax.random.randint(key_count, (blocks, half_leaves), 2, limits + 1, dtype=jnp.int32)
    full_row = jax.random.randint(key_full, (blocks, 1), 0, half_leaves, dtype=jnp.int32)
    drawn = jnp.where(jnp.arange(half_leaves, dtype=jnp.int32)[None, :] == full_row, NEAR, drawn)
    return drawn.reshape(LEAVES).astype(jnp.int32)


def draw_box_list(key, part):
    key = jax.random.fold_in(key, 13)
    half_boxes = GROUP_LEAVES // 16
    blocks = BOXES // half_boxes
    key_rest, key_order = jax.random.split(key, 2)
    random_rows = jax.random.randint(key_rest, (blocks, half_boxes, F1), 0, 3 * BOX_GROUP, dtype=jnp.int32)
    shuffled = jax.vmap(lambda subkey: jax.random.permutation(subkey, 2 * BOX_GROUP))(jax.random.split(key_order, blocks)).astype(jnp.int32)
    shuffled = shuffled.reshape(blocks, half_boxes, 4)
    rows = random_rows.at[:, :, 0:4].set(BOX_GROUP + shuffled)
    return rows.reshape(BOXES, F1)


def draw_root_list(key, part):
    key = jax.random.fold_in(key, 14)
    shuffled = jax.vmap(lambda subkey: jax.random.permutation(subkey, GROUPS - 1))(jax.random.split(key, GROUPS)).astype(jnp.int32)
    offsets = shuffled[:, :F2] + 1
    return ((jnp.arange(GROUPS, dtype=jnp.int32)[:, None] + offsets) % GROUPS).astype(jnp.int32)


def plant(values, rng, least, top_value):
    longest = values.shape.index(max(values.shape))
    spots = []
    for shift in (0, 1):
        where = [jax.random.randint(jax.random.fold_in(rng, axis), (), 0, length) for axis, length in enumerate(values.shape)]
        where[longest] = (where[longest] + shift) % values.shape[longest]
        spots.append(tuple(where))
    return values.at[spots[0]].set(least).at[spots[1]].set(top_value)


def level_of(own_key, extent, shards, smallest, largest):
    loudness = 1.0
    for dim, parts in shards:
        heights = jax.random.uniform(jax.random.fold_in(jax.random.fold_in(own_key, 6), dim), (parts,), jnp.float32, smallest / len(shards), largest / len(shards))
        loudness = loudness * jnp.repeat(jnp.exp(heights), extent[dim] // parts).reshape((-1,) + (1,) * (len(extent) - 1 - dim))
    return loudness


def noise(key, dims, scale, most, cuts=(), held_as=jnp.bfloat16):
    values = scale * jax.random.normal(key, dims, jnp.float32)
    if cuts:
        values = values * level_of(key, dims, cuts, -0.22, 0.18)
    return jnp.clip(values, -most, most).astype(held_as)


def setup_inputs(seed: int = 0) -> dict:
    seeds = jax.random.split(jax.random.key(seed), 14)
    return {
        "density": noise(seeds[0], (RHS, POINTS), 1.0, 6.0, ((1, 128),)),
        "coords": jnp.clip(1.0 * jax.random.uniform(seeds[1], (3, POINTS), jnp.float32) ** level_of(seeds[1], (3, POINTS), ((1, 128),), -0.2, 0.2), 0.0, 1.0),
        "qweight": jnp.clip(jnp.exp(math.log(0.08) - 2.0794415 * jax.random.uniform(seeds[2], (POINTS,), jnp.float32) ** level_of(seeds[2], (POINTS,), ((0, 128),), -0.2, 0.2)), 0.01, 0.08),
        "leaf_basis": noise(seeds[3], (LEAVES, LEAF * RANK), LEAF ** -0.5, 0.75, ((0, 128),)),
        "box_transfer": noise(seeds[4], (LEAVES, RANK * RANK), RANK ** -0.5, 0.75, ((0, 128),)),
        "root_transfer": noise(seeds[5], (BOXES, RANK * RANK), RANK ** -0.5, 0.75, ((0, 128),)),
        "box_coupling": noise(seeds[6], (BOXES, F1, RANK * RANK), (RANK // 4) ** -0.5, 1.5, ((0, 256),)),
        "root_coupling": noise(seeds[7], (GROUPS, F2, RANK * RANK), RANK ** -0.5, 0.75, ((0, 128),)),
        "near_list": draw_near_list(jax.random.fold_in(seeds[13], 71), 0),
        "near_count": draw_near_count(jax.random.fold_in(seeds[13], 71), 0),
        "box_list": draw_box_list(jax.random.fold_in(seeds[13], 71), 0),
        "root_list": draw_root_list(jax.random.fold_in(seeds[13], 71), 0),
        "ghost_send": plant(jax.random.randint(seeds[12], (GROUPS, 2, 2, GHOST), 0, GROUP_LEAVES), jax.random.fold_in(seeds[12], 1), 0, GROUP_LEAVES - 1).astype(jnp.int32),
    }


DELTA_SQ = 0.0025
FULL_PRECISION = lax.Precision.HIGHEST

def kernel_block(targets, sources):
    offsets = targets[:, :, :, None] - sources[:, :, None, :]
    distance = lax.optimization_barrier(jnp.sum(offsets * offsets, axis=0))
    return (1.0 / jnp.sqrt(distance + DELTA_SQ)).astype(jnp.bfloat16)

def reference(density, coords, qweight, leaf_basis, box_transfer, root_transfer, box_coupling, root_coupling, near_list, near_count, box_list, root_list, ghost_send):
    half_leaves = GROUP_LEAVES // 2
    weighted = (density.astype(jnp.float32) * qweight[None, :]).astype(jnp.bfloat16)
    weighted_leaf = weighted.reshape(RHS, LEAVES, LEAF)
    basis_cube = leaf_basis.reshape(LEAVES, LEAF, RANK).astype(jnp.float32)
    leaf_coefs = jnp.einsum('lpa,qlp->laq', basis_cube, weighted_leaf.astype(jnp.float32), precision=FULL_PRECISION).astype(jnp.bfloat16)
    up_leaf = box_transfer.reshape(LEAVES, RANK, RANK).astype(jnp.float32)
    box_coefs = jnp.einsum('lac,laq->lcq', up_leaf, leaf_coefs.astype(jnp.float32), precision=FULL_PRECISION).reshape(BOXES, 8, RANK, RHS).sum(axis=1).astype(jnp.bfloat16)
    up_box = root_transfer.reshape(BOXES, RANK, RANK).astype(jnp.float32)
    root_coefs = jnp.einsum('bac,baq->bcq', up_box, box_coefs.astype(jnp.float32), precision=FULL_PRECISION).reshape(GROUPS, BOX_GROUP, RANK, RHS).sum(axis=1).astype(jnp.bfloat16)
    picked = root_coefs[root_list].astype(jnp.float32)
    top_coupling = root_coupling.reshape(GROUPS, F2, RANK, RANK).astype(jnp.float32)
    root_fields = jnp.einsum('gkac,gkcq->gaq', top_coupling, picked, precision=FULL_PRECISION).astype(jnp.bfloat16)
    box_group = jnp.arange(BOXES, dtype=jnp.int32) // BOX_GROUP
    box_fields = jnp.einsum('bac,bcq->baq', up_box, root_fields[box_group].astype(jnp.float32), precision=FULL_PRECISION)
    couple = box_coupling.reshape(BOXES, F1, RANK, RANK)
    box_wide = box_coefs.astype(jnp.float32)
    for column in range(F1):
        entries = box_list[:, column]
        region = entries // BOX_GROUP
        source_group = box_group + jnp.where(region == 1, -1, jnp.where(region == 2, 1, 0)).astype(jnp.int32)
        counted = (source_group >= 0) & (source_group < GROUPS)
        source = (jnp.clip(source_group, 0, GROUPS - 1) * BOX_GROUP + entries % BOX_GROUP).astype(jnp.int32)
        contribution = jnp.einsum('bac,bcq->baq', couple[:, column].astype(jnp.float32), box_wide[source], precision=FULL_PRECISION)
        box_fields = box_fields + jnp.where(counted[:, None, None], contribution, 0.0)
    box_fields = box_fields.astype(jnp.bfloat16)
    leaf_box = jnp.arange(LEAVES, dtype=jnp.int32) // 8
    leaf_fields = jnp.einsum('lac,lcq->laq', up_leaf, box_fields[leaf_box].astype(jnp.float32), precision=FULL_PRECISION).astype(jnp.bfloat16)
    far_part = jnp.einsum('lpa,laq->qlp', basis_cube, leaf_fields.astype(jnp.float32), precision=FULL_PRECISION)
    coords_leaf = coords.reshape(3, LEAVES, LEAF)

    def near_half(block_index):
        group_index = block_index // 2
        half_index = block_index % 2
        first_leaf = block_index * half_leaves
        targets = lax.dynamic_slice_in_dim(coords_leaf, first_leaf, half_leaves, 1)
        near_rows = lax.dynamic_slice_in_dim(near_list, first_leaf, half_leaves, 0)
        counts = lax.dynamic_slice_in_dim(near_count, first_leaf, half_leaves, 0)
        group_below = jnp.clip(group_index - 1, 0, GROUPS - 1)
        group_above = jnp.clip(group_index + 1, 0, GROUPS - 1)
        accum = jnp.zeros((RHS, half_leaves, LEAF), jnp.float32)
        for column in range(NEAR):
            entries = near_rows[:, column]
            is_low = (entries >= GROUP_LEAVES) & (entries < GROUP_LEAVES + GHOST)
            is_high = entries >= GROUP_LEAVES + GHOST
            low_leaf = group_below * GROUP_LEAVES + ghost_send[group_below, half_index, 0, jnp.clip(entries - GROUP_LEAVES, 0, GHOST - 1)]
            high_leaf = group_above * GROUP_LEAVES + ghost_send[group_above, half_index, 1, jnp.clip(entries - GROUP_LEAVES - GHOST, 0, GHOST - 1)]
            own_leaf = group_index * GROUP_LEAVES + jnp.clip(entries, 0, GROUP_LEAVES - 1)
            source = jnp.where(is_high, high_leaf, jnp.where(is_low, low_leaf, own_leaf)).astype(jnp.int32)
            counted = (column < counts) & ~(is_low & (group_index == 0)) & ~(is_high & (group_index == GROUPS - 1))
            kernel = kernel_block(targets, coords_leaf[:, source, :])
            contribution = jnp.einsum('hij,qhj->qhi', kernel.astype(jnp.float32), weighted_leaf[:, source, :].astype(jnp.float32), precision=FULL_PRECISION)
            accum = accum + jnp.where(counted[None, :, None], contribution, 0.0)
        return accum
    near_blocks = lax.map(near_half, jnp.arange(2 * GROUPS, dtype=jnp.int32))
    near_part = jnp.transpose(near_blocks, (1, 0, 2, 3)).reshape(RHS, POINTS)
    return (far_part.reshape(RHS, POINTS) + near_part).astype(jnp.bfloat16)
```

```python
import functools

import jax
import jax.numpy as jnp
import numpy as np
from jax import lax
from jax.experimental import pallas as pl
from jax.experimental.pallas import tpu as pltpu
from jax.sharding import PartitionSpec as P

LEAF = 64
RANK = 64
DELTA_SQ = 0.0025
F32 = jnp.float32
BF16 = jnp.bfloat16
VMEM = pltpu.VMEM
NT = (((1,), (1,)), ((), ()))


def in_order_matrix():
    out = np.zeros((512, 512), np.float32)
    for leaf in range(8):
        for m in range(32):
            for par in range(2):
                out[leaf * 64 + 2 * m + par, par * 256 + m * 8 + leaf] = 1
    return out


def unfold_matrix():
    out = np.zeros((512, 128), np.float32)
    for par in range(2):
        for m in range(32):
            for leaf in range(8):
                out[par * 256 + m * 8 + leaf, 2 * m + par] = 1
                out[par * 256 + m * 8 + leaf, 64 + 2 * m + par] = 1
    return out


def spread_matrix():
    out = unfold_matrix().T.copy()
    out[64:] = 0
    return out


def dot(a, b):
    return jnp.dot(a, b, preferred_element_type=F32)


def dot_t(a, b):
    return lax.dot_general(a, b, NT, preferred_element_type=F32)


def low_half(shape):
    return lax.broadcasted_iota(jnp.int32, shape, len(shape) - 1) < 64


def lane_slot(shape):
    return lax.broadcasted_iota(jnp.int32, shape, len(shape) - 1) & 7


def roll_half(value):
    return pltpu.roll(value, 64, value.ndim - 1)


def half_masks():
    low = low_half((16, 128))
    return (
        jnp.where(low, 1.0, 0.0).astype(BF16),
        jnp.where(low, 0.0, 1.0).astype(BF16),
    )


def slot_masks(rows):
    slot = lane_slot((rows, 256))
    return [jnp.where(slot == s, 1.0, 0.0).astype(BF16) for s in range(8)]


def pick_slots(parts):
    slot = lane_slot(parts[0].shape)
    out = parts[0]
    for s in range(1, 8):
        out = jnp.where(slot == s, parts[s], out)
    return out


def add_halves(value):
    chosen = jnp.where(low_half((16, 128)), value[:16], value[16:])
    return chosen + roll_half(chosen)


def spread(coefs, spread_ref):
    wide = dot(coefs, spread_ref[...])
    picked = pick_slots([wide[s * 16 : s * 16 + 16] for s in range(8)]).astype(BF16)
    return jnp.concatenate([picked[:, :256], picked[:, 256:]], axis=0)


def up_kernel(
    send,
    dens,
    qw,
    coords,
    basis,
    trans,
    rtrans,
    order,
    spread_ref,
    zw,
    pay_low,
    pay_high,
    boxes,
    root,
    flat,
    ordered,
    cz,
    rolled,
):
    tiles = dens.shape[1] // 128
    box_count = tiles // 4
    mlo, mhi = half_masks()

    def weigh(b, carry):
        at = pl.multiple_of(b * 512, 512)
        row = pl.multiple_of(b * 16, 16)
        w = (dens[:, pl.ds(at, 512)].astype(F32) * qw[:, pl.ds(at, 512)]).astype(BF16)
        flat[pl.ds(row, 16), :] = w
        wide = w.astype(F32)
        c = coords[:, pl.ds(at, 512)]
        c = jnp.concatenate([c, jnp.zeros((5, 512), F32)], axis=0)
        for j in range(4):
            v = b * 4 + j
            cut = slice(j * 128, j * 128 + 128)
            zw[v] = w[:, cut]
            rolled[v] = w[:, cut]
            rolled[tiles + v] = roll_half(wide[:, cut]).astype(BF16)
            cz[v] = c[:, cut]
            cz[tiles + v] = roll_half(c[:, cut])
        return carry

    lax.fori_loop(0, box_count, weigh, 0, unroll=2)

    ordered[...] = dot(flat[...], order[...]).astype(BF16)

    low8 = low_half((8, 128))

    def pack(i, carry):
        for d, pay in ((0, pay_low), (1, pay_high)):
            parts = []
            for j in range(2):
                pair = i * 2 + j
                s0 = send[d * 64 + pair * 2]
                s1 = send[d * 64 + pair * 2 + 1]
                i0 = (s0 >> 1) + tiles * (s0 & 1)
                i1 = (s1 >> 1) + tiles * (1 - (s1 & 1))
                pay[pl.ds(pl.multiple_of(pair * 16, 16), 16), :] = (
                    rolled[i0] * mlo + rolled[i1] * mhi
                )
                c = jnp.where(low8, cz[i0], cz[i1])
                high = c.astype(BF16).astype(F32)
                parts += [high[0:4], (c - high)[0:4]]
            pay[pl.ds(pl.multiple_of(512 + i * 16, 16), 16), :] = jnp.concatenate(
                parts, axis=0
            ).astype(BF16)
        return carry

    lax.fori_loop(0, 16, pack, 0, unroll=2)

    masks = slot_masks(32)

    def up(b, carry):
        rows = pl.ds(pl.multiple_of(b * 256, 256), 256)
        w = ordered[pl.ds(pl.multiple_of(b * 16, 16), 16), :]
        w = jnp.concatenate([w[:, :256], w[:, 256:]], axis=0)
        moving = jnp.concatenate([w * m for m in masks], axis=0)
        out = dot(moving, basis[rows, :])
        coefs = jnp.concatenate(
            [add_halves(out[s * 32 : s * 32 + 32]) for s in range(8)], axis=0
        ).astype(BF16)
        total = dot(spread(coefs, spread_ref), trans[rows, :])
        boxes[b] = add_halves(total).astype(BF16)
        return carry

    lax.fori_loop(0, box_count, up, 0, unroll=4)

    def finish(i, carry):
        pair = boxes[2 * i] * mlo + boxes[2 * i + 1] * mhi
        rows = pl.ds(pl.multiple_of(768 + i * 16, 16), 16)
        pay_low[rows, :] = pair
        pay_high[rows, :] = pair
        return carry

    lax.fori_loop(0, box_count // 2, finish, 0, unroll=4)

    total = jnp.zeros((32, 128), F32)
    for g in range(box_count // 8):
        coefs = jnp.concatenate([boxes[g * 8 + s] for s in range(8)], axis=0)
        total += dot(spread(coefs, spread_ref), rtrans[g * 256 : g * 256 + 256, :])
    top = add_halves(total)
    root[...] = jnp.where(low8, top[:8], top[8:]).astype(BF16)


def split3(value):
    high = value.astype(BF16).astype(F32)
    rest = value - high
    mid = rest.astype(BF16).astype(F32)
    return high, mid, rest - mid


def near_kernel(
    where,
    near,
    slots,
    groups,
    box_list,
    zw,
    coords,
    pay_below,
    pay_above,
    boxes,
    coup,
    near_out,
    fields,
    feats,
    wz,
    tt,
    acc,
    ab,
):
    own_tiles = zw.shape[0]
    ghost = 32
    tiles = own_tiles + 2 * ghost + 1
    half_tiles = own_tiles // 2
    mlo, mhi = half_masks()
    low8 = low_half((8, 128))
    row8 = lax.broadcasted_iota(jnp.int32, (8, 128), 0)

    def put_source(v, c, w):
        c = jnp.where(row8 < 3, c - 0.5, 0.0)
        size = jnp.sum(c * c, axis=0, keepdims=True)
        u = jnp.where(row8 < 3, c, jnp.where(row8 == 3, size, jnp.where(row8 == 4, 1.0, 0.0)))
        for at, block in ((v, u), (tiles + v, roll_half(u))):
            h, m, l = split3(block)
            feats[at] = jnp.concatenate([h, m, l, h, m, h], axis=0).astype(BF16)
        wz[v] = w
        wz[tiles + v] = roll_half(w.astype(F32)).astype(BF16)
        return c, size

    def own(i, carry):
        for j in range(4):
            v = i * 4 + j
            c = coords[:, pl.ds(pl.multiple_of(v * 128, 128), 128)]
            c = jnp.concatenate([c, jnp.zeros((5, 128), F32)], axis=0)
            put_source(v, c, zw[v])
        return carry

    lax.fori_loop(0, own_tiles // 4, own, 0)

    eye = jnp.where(
        lax.broadcasted_iota(jnp.int32, (128, 128), 0)
        == lax.broadcasted_iota(jnp.int32, (128, 128), 1),
        1.0,
        0.0,
    ).astype(BF16)
    first_tile = where[0] * half_tiles

    def target(i, carry):
        for j in range(4):
            v = i * 4 + j
            c = coords[:, pl.ds(pl.multiple_of((first_tile + v) * 128, 128), 128)]
            c = jnp.concatenate([c, jnp.zeros((5, 128), F32)], axis=0)
            c = jnp.where(row8 < 3, c - 0.5, 0.0)
            size = jnp.sum(c * c, axis=0, keepdims=True) + DELTA_SQ
            u = jnp.where(
                row8 < 3, -2.0 * c, jnp.where(row8 == 3, 1.0, jnp.where(row8 == 4, size, 0.0))
            )
            h, m, l = split3(u)
            block = jnp.concatenate([h, h, h, m, m, l], axis=0).astype(BF16)
            tt[pl.ds(pl.multiple_of(v * 128, 128), 128), :] = dot_t(eye, block).astype(BF16)
        return carry

    lax.fori_loop(0, half_tiles // 4, target, 0)
    tt[pl.ds(half_tiles * 128, 64), :] = jnp.zeros((64, 48), BF16)

    for base, pay in ((own_tiles, pay_below), (own_tiles + ghost, pay_above)):

        def ghosts(i, carry, base=base, pay=pay):
            both = pay[pl.ds(pl.multiple_of(512 + i * 16, 16), 16), :].astype(F32)
            for j in range(2):
                v = i * 2 + j
                c = both[j * 8 : j * 8 + 4] + both[j * 8 + 4 : j * 8 + 8]
                c = jnp.concatenate([c, jnp.zeros((4, 128), F32)], axis=0)
                put_source(base + v, c, pay[pl.ds(pl.multiple_of(v * 16, 16), 16), :])
            return carry

        lax.fori_loop(0, ghost // 2, ghosts, 0, unroll=2)

    put_source(tiles - 1, jnp.zeros((8, 128), F32), jnp.zeros((16, 128), BF16))

    def clear(i, carry):
        acc[i] = jnp.zeros((16, 64), F32)
        return carry

    lax.fori_loop(0, 2 * half_tiles + 1, clear, 0, unroll=8)

    def block(slot):
        v = slots[slot]
        t = v >> 3
        at = t * 12 + (v & 7) * 2
        e0 = near[at]
        e1 = near[at + 1]
        i0 = (e0 >> 1) + tiles * (e0 & 1)
        i1 = (e1 >> 1) + tiles * (1 - (e1 & 1))
        f0 = feats[i0]
        f1 = feats[i1]
        source = jnp.concatenate(
            [f0[r : r + 16] * mlo + f1[r : r + 16] * mhi for r in (0, 16, 32)], axis=0
        )
        w = wz[i0] * mlo + wz[i1] * mhi
        square = dot(tt[pl.ds(pl.multiple_of(t * 64, 64), 64), :], source)
        return t, dot_t(w, lax.rsqrt(square).astype(BF16))

    def items(i, carry):
        done = [block(i * 8 + j) for j in range(8)]
        for t, value in done:
            acc[t] += value
        return carry

    lax.fori_loop(0, groups[0], items, 0)

    def join(v, carry):
        near_out[v] = jnp.concatenate([acc[2 * v], acc[2 * v + 1]], axis=1)
        return carry

    lax.fori_loop(0, half_tiles, join, 0, unroll=4)

    own_boxes = boxes.shape[0]

    def own_box(i, carry):
        ab[i] = boxes[i]
        return carry

    lax.fori_loop(0, own_boxes, own_box, 0, unroll=4)
    low16 = low_half((16, 128))
    for base, pay in ((own_boxes, pay_below), (2 * own_boxes, pay_above)):

        def ghost_box(i, carry, base=base, pay=pay):
            pair = pay[pl.ds(pl.multiple_of(768 + i * 16, 16), 16), :].astype(F32)
            turned = roll_half(pair)
            ab[base + 2 * i] = jnp.where(low16, pair, turned).astype(BF16)
            ab[base + 2 * i + 1] = jnp.where(low16, turned, pair).astype(BF16)
            return carry

        lax.fori_loop(0, own_boxes // 2, ghost_box, 0, unroll=4)

    def couple(b, carry):
        total = None
        for kg in range(2):
            rows = []
            for k in range(8):
                source = ab[box_list[b * 16 + kg * 8 + k]]
                rows += [source * mlo, source * mhi]
            at = pl.ds(pl.multiple_of((b * 2 + kg) * 256, 256), 256)
            wide = dot_t(jnp.concatenate(rows, axis=0), coup[at, :])
            part = pick_slots([wide[s * 32 : s * 32 + 32] for s in range(8)])
            total = part if total is None else total + part
        fields[b] = total
        return carry

    lax.fori_loop(0, fields.shape[0], couple, 0, unroll=2)


def fold(parts, unfold):
    rows = [jnp.concatenate([p[:16], p[16:]], axis=1) for p in parts]
    high = [r.astype(BF16) for r in rows]
    low = [(r - h.astype(F32)).astype(BF16) for r, h in zip(rows, high)]
    out = dot(jnp.concatenate(high + low, axis=0), unfold[...])
    n = 16 * len(parts)
    return out[:n] + out[n:]


def down_kernel(
    where,
    root_list,
    roots,
    rcoup,
    rtrans,
    fields,
    trans,
    basis,
    near,
    unfold,
    back,
    out,
    bf,
    far_high,
    far_low,
):
    mlo, mhi = half_masks()
    low8 = low_half((8, 128))
    half_boxes = fields.shape[0]

    total = None
    for kg in range(2):
        rows = []
        for k in range(8):
            if kg * 8 + k < 12:
                source = roots[root_list[kg * 8 + k]].astype(F32)
                turned = roll_half(source)
                even = jnp.concatenate([source, turned], axis=0).astype(BF16) * mlo
                odd = jnp.concatenate([turned, source], axis=0).astype(BF16) * mhi
                rows += [even, odd]
            else:
                rows.append(jnp.zeros((32, 128), BF16))
        wide = dot_t(jnp.concatenate(rows, axis=0), rcoup[kg * 256 : kg * 256 + 256, :])
        part = pick_slots([wide[s * 32 : s * 32 + 32] for s in range(8)])
        total = part if total is None else total + part
    rf = fold([total], unfold).astype(BF16)
    moving = jnp.concatenate([rf * mlo, rf * mhi], axis=0)
    slot = lane_slot((32, 256))
    for g in range(half_boxes // 8):
        pushed = dot_t(moving, rtrans[g * 256 : g * 256 + 256, :])
        sums = [fields[g * 8 + s] + jnp.where(slot == s, pushed, 0.0) for s in range(8)]
        bf[g * 128 : g * 128 + 128, :] = fold(sums, unfold).astype(BF16)

    masks = slot_masks(16)

    def leaves(b, carry):
        rows = pl.ds(pl.multiple_of(b * 256, 256), 256)
        at = pl.ds(pl.multiple_of(b * 16, 16), 16)
        field = bf[at, :]
        h = dot_t(jnp.concatenate([field * mlo, field * mhi], axis=0), trans[rows, :])
        h = h.astype(BF16)
        wide = jnp.concatenate(
            [jnp.concatenate([h[:16] * m, h[16:] * m], axis=1) for m in masks], axis=0
        )
        lf = dot(wide, unfold[...]).astype(BF16)
        parts = []
        for s in range(8):
            one = lf[s * 16 : s * 16 + 16]
            parts += [one * mlo, one * mhi]
        far = dot_t(jnp.concatenate(parts, axis=0), basis[rows, :])
        far = pick_slots([far[s * 32 : s * 32 + 32] for s in range(8)])
        far = jnp.concatenate([far[:16], far[16:]], axis=1)
        high = far.astype(BF16)
        far_high[at, :] = high
        far_low[at, :] = (far - high.astype(F32)).astype(BF16)
        return carry

    lax.fori_loop(0, half_boxes, leaves, 0, unroll=2)

    def emit(i, carry):
        at = pl.ds(pl.multiple_of(i * 64, 64), 64)
        far = dot(far_high[at, :], back[...]) + dot(far_low[at, :], back[...])
        for b in range(4):
            for j in range(4):
                v = (i * 4 + b) * 4 + j
                value = far[b * 16 : b * 16 + 16, j * 128 : j * 128 + 128] + near[v]
                out[:, pl.ds(pl.multiple_of(v * 128, 128), 128)] = value.astype(BF16)
        return carry

    lax.fori_loop(0, half_boxes // 4, emit, 0)


def natural(matrices):
    n = matrices.shape[0]
    return jnp.transpose(matrices.reshape(n // 8, 8, 32, 128), (0, 2, 1, 3)).reshape(n * 32, 128)


def whole(shape=None):
    return pl.BlockSpec(memory_space=VMEM)


def smem():
    return pl.BlockSpec(memory_space=pltpu.SMEM)


def shape_of(shape, dtype):
    return jax.ShapeDtypeStruct(shape, dtype)


def params():
    return pltpu.CompilerParams(vmem_limit_bytes=40 * 1024 * 1024)


def shifted(value, by):
    peers = lax.axis_size("leaf")
    pairs = [(i, i + by) for i in range(peers) if 0 <= i + by < peers]
    return lax.ppermute(value, "leaf", pairs)


def gather_roots(root):
    peers = lax.axis_size("leaf")
    copies = jnp.broadcast_to(root[None], (peers,) + root.shape)
    return lax.all_to_all(copies, "leaf", 0, 0, tiled=True)


def per_device(
    density,
    coords,
    qweight,
    leaf_basis,
    box_transfer,
    root_transfer,
    box_coupling,
    root_coupling,
    near_list,
    near_count,
    box_list,
    root_list,
    ghost_send,
):
    points = density.shape[1]
    tiles = points // 128
    box_count = tiles // 4
    half_leaves = near_list.shape[0]
    half_boxes = box_list.shape[0]
    where = lax.axis_index("sub").astype(jnp.int32).reshape(1)
    basis = natural(leaf_basis)
    trans = natural(box_transfer)
    rtrans = natural(root_transfer)
    coup = natural(box_coupling.reshape(half_boxes * 16, 4096))
    rcoup = natural(jnp.pad(root_coupling[0], ((0, 4), (0, 0))))
    order = jnp.asarray(in_order_matrix(), BF16)
    back = jnp.asarray(in_order_matrix().T.copy(), BF16)
    spread_m = jnp.asarray(spread_matrix(), BF16)
    unfold = jnp.asarray(unfold_matrix(), BF16)

    zw, pay_low, pay_high, boxes, root = pl.pallas_call(
        up_kernel,
        name="up",
        out_shape=(
            shape_of((tiles, 16, 128), BF16),
            shape_of((1024, 128), BF16),
            shape_of((1024, 128), BF16),
            shape_of((box_count, 16, 128), BF16),
            shape_of((8, 128), BF16),
        ),
        in_specs=[smem()] + [whole()] * 8,
        out_specs=tuple([whole()] * 5),
        scratch_shapes=[
            VMEM((box_count * 16, 512), BF16),
            VMEM((box_count * 16, 512), BF16),
            VMEM((2 * tiles, 8, 128), F32),
            VMEM((2 * tiles, 16, 128), BF16),
        ],
        compiler_params=params(),
    )(
        ghost_send.reshape(-1),
        density,
        qweight.reshape(1, points),
        coords,
        basis,
        trans,
        rtrans,
        order,
        spread_m,
    )
    pay_below = shifted(pay_low, 1)
    pay_above = shifted(pay_high, -1)
    roots = gather_roots(root)

    live = lax.broadcasted_iota(jnp.int32, near_list.shape, 1) < near_count[:, None]
    entries = jnp.where(live, near_list, 2 * tiles + 128)
    entries = jnp.pad(entries, ((0, 1), (0, 0)), constant_values=2 * tiles + 128).reshape(-1)
    pairs = (near_count + 1) // 2
    index = jnp.arange(half_leaves, dtype=jnp.int32)
    ends = jnp.sum(jnp.where(index[None, :] <= index[:, None], pairs[None, :], 0), axis=1)
    slot = jnp.arange(half_leaves * 6 + 8, dtype=jnp.int32)
    passed = ends[None, :] <= slot[:, None]
    target = jnp.sum(passed.astype(jnp.int32), axis=1)
    begin = jnp.max(jnp.where(passed, ends[None, :], 0), axis=1)
    slots = jnp.where(target < half_leaves, target * 8 + slot - begin, half_leaves * 8)
    groups = ((ends[-1:] + 7) // 8).astype(jnp.int32)

    table = 2 * (tiles + 65)
    near, fields = pl.pallas_call(
        near_kernel,
        name="near",
        out_shape=(
            shape_of((half_leaves // 2, 16, 128), F32),
            shape_of((half_boxes, 32, 256), F32),
        ),
        in_specs=[smem()] * 5 + [whole()] * 6,
        out_specs=(whole(), whole()),
        scratch_shapes=[
            VMEM((table, 48, 128), BF16),
            VMEM((table, 16, 128), BF16),
            VMEM(((half_leaves + 1) * 64, 48), BF16),
            VMEM((half_leaves + 1, 16, 64), F32),
            VMEM((3 * box_count, 16, 128), BF16),
        ],
        compiler_params=params(),
        cost_estimate=pl.CostEstimate(flops=10**9, bytes_accessed=10**7, transcendentals=6 * 10**6),
    )(
        where,
        entries,
        slots,
        groups,
        box_list.reshape(-1),
        zw,
        coords,
        pay_below,
        pay_above,
        boxes,
        coup,
    )

    def all_of(shape):
        return pl.BlockSpec(shape, lambda i, w, r: (0,) * len(shape))

    def own_half(rows):
        return pl.BlockSpec((rows, 128), lambda i, w, r: (w[0], 0))

    return pl.pallas_call(
        down_kernel,
        name="down",
        out_shape=shape_of((16, half_leaves * 64), BF16),
        grid_spec=pltpu.PrefetchScalarGridSpec(
            num_scalar_prefetch=2,
            grid=(1,),
            in_specs=[
                all_of(roots.shape),
                all_of(rcoup.shape),
                own_half(half_boxes * 32),
                all_of(fields.shape),
                own_half(half_leaves * 32),
                own_half(half_leaves * 32),
                all_of(near.shape),
                all_of(unfold.shape),
                all_of(back.shape),
            ],
            out_specs=all_of((16, half_leaves * 64)),
            scratch_shapes=[
                VMEM((half_boxes * 16, 128), BF16),
                VMEM((half_boxes * 16, 512), BF16),
                VMEM((half_boxes * 16, 512), BF16),
            ],
        ),
        compiler_params=params(),
    )(where, root_list.reshape(-1), roots, rcoup, rtrans, fields, trans, basis, near, unfold, back)


def solution(mesh):
    in_specs = (
        P(None, "leaf"),
        P(None, "leaf"),
        P("leaf"),
        P("leaf", None),
        P("leaf", None),
        P("leaf", None),
        P(("leaf", "sub"), None, None),
        P("leaf", None, None),
        P(("leaf", "sub"), None),
        P(("leaf", "sub")),
        P(("leaf", "sub"), None),
        P("leaf", None),
        P("leaf", "sub", None, None),
    )
    out_specs = P(None, ("leaf", "sub"))
    return jax.shard_map(
        per_device, mesh=mesh, in_specs=in_specs, out_specs=out_specs, check_vma=False
    )
```

```python
import functools

import jax
import jax.numpy as jnp
import numpy as np
from jax import lax
from jax.experimental import pallas as pl
from jax.experimental.pallas import tpu as pltpu
from jax.sharding import PartitionSpec as P

LEAF = 64
RANK = 64
DELTA_SQ = 0.0025
UP = 8
ITEMS = 8
DOWN = 4
F32 = jnp.float32
BF16 = jnp.bfloat16
VMEM = pltpu.VMEM
NT = (((1,), (1,)), ((), ()))


def in_order_matrix():
    out = np.zeros((512, 512), np.float32)
    for leaf in range(8):
        for m in range(32):
            for par in range(2):
                out[leaf * 64 + 2 * m + par, par * 256 + m * 8 + leaf] = 1
    return out


def unfold_matrix():
    out = np.zeros((512, 128), np.float32)
    for par in range(2):
        for m in range(32):
            for leaf in range(8):
                out[par * 256 + m * 8 + leaf, 2 * m + par] = 1
                out[par * 256 + m * 8 + leaf, 64 + 2 * m + par] = 1
    return out


def spread_matrix():
    out = unfold_matrix().T.copy()
    out[64:] = 0
    return out


def dot(a, b):
    return jnp.dot(a, b, preferred_element_type=F32)


def dot_t(a, b):
    return lax.dot_general(a, b, NT, preferred_element_type=F32)


def low_half(shape):
    return lax.broadcasted_iota(jnp.int32, shape, len(shape) - 1) < 64


def lane_slot(shape):
    return lax.broadcasted_iota(jnp.int32, shape, len(shape) - 1) & 7


def roll_half(value):
    return pltpu.roll(value, 64, value.ndim - 1)


def half_masks():
    low = low_half((16, 128))
    return (
        jnp.where(low, 1.0, 0.0).astype(BF16),
        jnp.where(low, 0.0, 1.0).astype(BF16),
    )


def slot_masks(rows):
    slot = lane_slot((rows, 256))
    return [jnp.where(slot == s, 1.0, 0.0).astype(BF16) for s in range(8)]


def pick_slots(parts):
    slot = lane_slot(parts[0].shape)
    out = parts[0]
    for s in range(1, 8):
        out = jnp.where(slot == s, parts[s], out)
    return out


def add_halves(value):
    chosen = jnp.where(low_half((16, 128)), value[:16], value[16:])
    return chosen + roll_half(chosen)


def gathered(wide):
    picked = pick_slots([wide[s * 16 : s * 16 + 16] for s in range(8)]).astype(BF16)
    return jnp.concatenate([picked[:, :256], picked[:, 256:]], axis=0)


def copied(pairs, sems):
    copies = [pltpu.make_async_copy(a, b, sems.at[i]) for i, (a, b) in enumerate(pairs)]
    for copy in copies:
        copy.start()
    return copies


def up_kernel(
    send,
    dens_in,
    qw_in,
    coords_in,
    basis_in,
    trans_in,
    rtrans_in,
    order_in,
    spread_in,
    zw_out,
    pay_low_out,
    pay_high_out,
    boxes_out,
    root_out,
    dens,
    qw,
    coords,
    basis,
    trans,
    rtrans,
    order,
    spread_ref,
    flat,
    ordered,
    cz,
    rolled,
    pay_low,
    pay_high,
    boxes,
    root,
    sems,
    out_sems,
):
    sources = (dens_in, qw_in, coords_in, order_in, basis_in, spread_in, trans_in, rtrans_in)
    places = (dens, qw, coords, order, basis, spread_ref, trans, rtrans)
    copies = copied(zip(sources, places), sems)
    for copy in copies[:3]:
        copy.wait()
    tiles = dens.shape[1] // 128
    box_count = tiles // 4
    mlo, mhi = half_masks()

    def weigh(b, carry):
        at = pl.multiple_of(b * 512, 512)
        row = pl.multiple_of(b * 16, 16)
        w = (dens[:, pl.ds(at, 512)].astype(F32) * qw[:, pl.ds(at, 512)]).astype(BF16)
        flat[pl.ds(row, 16), :] = w
        wide = w.astype(F32)
        c = coords[:, pl.ds(at, 512)]
        c = jnp.concatenate([c, jnp.zeros((5, 512), F32)], axis=0)
        for j in range(4):
            v = b * 4 + j
            cut = slice(j * 128, j * 128 + 128)
            rolled[v] = w[:, cut]
            rolled[tiles + v] = roll_half(wide[:, cut]).astype(BF16)
            cz[v] = c[:, cut]
            cz[tiles + v] = roll_half(c[:, cut])
        return carry

    lax.fori_loop(0, box_count, weigh, 0, unroll=2)

    kept = pltpu.make_async_copy(rolled.at[pl.ds(0, tiles)], zw_out, out_sems.at[0])
    kept.start()
    copies[3].wait()
    ordered[...] = dot(flat[...], order[...]).astype(BF16)

    low8 = low_half((8, 128))

    def pack(i, carry):
        for d, pay in ((0, pay_low), (1, pay_high)):
            parts = []
            for j in range(2):
                pair = i * 2 + j
                s0 = send[d * 64 + pair * 2]
                s1 = send[d * 64 + pair * 2 + 1]
                i0 = (s0 >> 1) + tiles * (s0 & 1)
                i1 = (s1 >> 1) + tiles * (1 - (s1 & 1))
                pay[pair] = rolled[i0] * mlo + rolled[i1] * mhi
                c = jnp.where(low8, cz[i0], cz[i1])
                high = c.astype(BF16).astype(F32)
                parts += [high[0:4], (c - high)[0:4]]
            pay[32 + i] = jnp.concatenate(parts, axis=0).astype(BF16)
        return carry

    lax.fori_loop(0, 16, pack, 0, unroll=2)

    masks = slot_masks(32)

    for copy in copies[4:]:
        copy.wait()

    def up(i, carry):
        picks = [i * UP + j for j in range(UP)]
        rows = [pl.ds(pl.multiple_of(b * 256, 256), 256) for b in picks]
        outs = []
        for b, r in zip(picks, rows):
            w = ordered[pl.ds(pl.multiple_of(b * 16, 16), 16), :]
            w = jnp.concatenate([w[:, :256], w[:, 256:]], axis=0)
            moving = jnp.concatenate([w * m for m in masks], axis=0)
            outs.append(dot(moving, basis[r, :]))
        coefs = [
            jnp.concatenate(
                [add_halves(out[s * 32 : s * 32 + 32]) for s in range(8)], axis=0
            ).astype(BF16)
            for out in outs
        ]
        wides = [dot(c, spread_ref[...]) for c in coefs]
        lifted = [dot(gathered(w), trans[r, :]) for w, r in zip(wides, rows)]
        for b, total in zip(picks, lifted):
            boxes[b] = add_halves(total).astype(BF16)
        return carry

    lax.fori_loop(0, box_count // UP, up, 0)

    def finish(i, carry):
        pair = boxes[2 * i] * mlo + boxes[2 * i + 1] * mhi
        pay_low[48 + i] = pair
        pay_high[48 + i] = pair
        return carry

    lax.fori_loop(0, box_count // 2, finish, 0, unroll=4)

    sends = [
        pltpu.make_async_copy(a, b, out_sems.at[i])
        for i, (a, b) in ((1, (pay_low, pay_low_out)), (2, (pay_high, pay_high_out)), (3, (boxes, boxes_out)))
    ]
    for copy in sends:
        copy.start()
    wides = [
        dot(jnp.concatenate([boxes[g * 8 + s] for s in range(8)], axis=0), spread_ref[...])
        for g in range(box_count // 8)
    ]
    total = jnp.zeros((32, 128), F32)
    for g, wide in enumerate(wides):
        total += dot(gathered(wide), rtrans[g * 256 : g * 256 + 256, :])
    top = add_halves(total)
    root[...] = jnp.where(low8, top[:8], top[8:]).astype(BF16)
    last = pltpu.make_async_copy(root, root_out, out_sems.at[4])
    last.start()
    for copy in sends + [kept, last]:
        copy.wait()


def split3(value):
    high = value.astype(BF16).astype(F32)
    rest = value - high
    mid = rest.astype(BF16).astype(F32)
    return high, mid, rest - mid


def near_kernel(
    where,
    near,
    slots,
    box_list,
    zw,
    coords_in,
    pay_below,
    pay_above,
    boxes,
    coup_in,
    near_hbm,
    fields_hbm,
    coords,
    extra_below,
    extra_above,
    coup,
    near_out,
    fields,
    feats,
    wz,
    tt,
    acc,
    ab,
    kernels,
    weights,
    sems,
    out_sems,
):
    own_tiles = zw.shape[0]
    ghost = 32
    tiles = own_tiles + 2 * ghost + 1
    half_tiles = own_tiles // 2
    mlo, mhi = half_masks()
    own_boxes = boxes.shape[0]
    copies = copied(
        (
            (coords_in, coords),
            (zw, wz.at[pl.ds(0, own_tiles)]),
            (pay_below.at[pl.ds(0, ghost)], wz.at[pl.ds(own_tiles, ghost)]),
            (pay_below.at[pl.ds(ghost, ghost)], extra_below),
            (pay_above.at[pl.ds(0, ghost)], wz.at[pl.ds(own_tiles + ghost, ghost)]),
            (pay_above.at[pl.ds(ghost, ghost)], extra_above),
            (boxes, ab.at[pl.ds(0, own_boxes)]),
            (coup_in, coup),
        ),
        sems,
    )
    copies[0].wait()
    row8 = lax.broadcasted_iota(jnp.int32, (8, 128), 0)

    def put_source(v, c):
        c = jnp.where(row8 < 3, c - 0.5, 0.0)
        size = jnp.sum(c * c, axis=0, keepdims=True)
        u = jnp.where(row8 < 3, c, jnp.where(row8 == 3, size, jnp.where(row8 == 4, 1.0, 0.0)))
        for at, block in ((v, u), (tiles + v, roll_half(u))):
            h, m, l = split3(block)
            feats[at] = jnp.concatenate([h, m, l, h, m, h], axis=0).astype(BF16)
        wz[tiles + v] = roll_half(wz[v].astype(F32)).astype(BF16)

    def own(i, carry):
        for j in range(8):
            v = i * 8 + j
            c = coords[:, pl.ds(pl.multiple_of(v * 128, 128), 128)]
            c = jnp.concatenate([c, jnp.zeros((5, 128), F32)], axis=0)
            put_source(v, c)
        return carry

    copies[1].wait()

    lax.fori_loop(0, own_tiles // 8, own, 0)

    eye = jnp.where(
        lax.broadcasted_iota(jnp.int32, (128, 128), 0)
        == lax.broadcasted_iota(jnp.int32, (128, 128), 1),
        1.0,
        0.0,
    ).astype(BF16)
    first_tile = where[0] * half_tiles

    def target(i, carry):
        blocks = []
        for j in range(8):
            v = i * 8 + j
            c = coords[:, pl.ds(pl.multiple_of((first_tile + v) * 128, 128), 128)]
            c = jnp.concatenate([c, jnp.zeros((5, 128), F32)], axis=0)
            c = jnp.where(row8 < 3, c - 0.5, 0.0)
            size = jnp.sum(c * c, axis=0, keepdims=True) + DELTA_SQ
            u = jnp.where(
                row8 < 3, -2.0 * c, jnp.where(row8 == 3, 1.0, jnp.where(row8 == 4, size, 0.0))
            )
            h, m, l = split3(u)
            blocks.append(jnp.concatenate([h, h, h, m, m, l], axis=0).astype(BF16))
        for j, turned in enumerate([dot_t(eye, block) for block in blocks]):
            tt[pl.ds(pl.multiple_of((i * 8 + j) * 128, 128), 128), :] = turned.astype(BF16)
        return carry

    lax.fori_loop(0, half_tiles // 8, target, 0)
    tt[pl.ds(half_tiles * 128, 64), :] = jnp.zeros((64, 48), BF16)

    for copy in copies[2:6]:
        copy.wait()
    for base, pay in ((own_tiles, extra_below), (own_tiles + ghost, extra_above)):

        def ghosts(i, carry, base=base, pay=pay):
            both = pay[i].astype(F32)
            for j in range(2):
                v = i * 2 + j
                c = both[j * 8 : j * 8 + 4] + both[j * 8 + 4 : j * 8 + 8]
                c = jnp.concatenate([c, jnp.zeros((4, 128), F32)], axis=0)
                put_source(base + v, c)
            return carry

        lax.fori_loop(0, ghost // 2, ghosts, 0, unroll=2)

    wz[tiles - 1] = jnp.zeros((16, 128), BF16)
    put_source(tiles - 1, jnp.zeros((8, 128), F32))

    def clear(i, carry):
        acc[i] = jnp.zeros((16, 64), F32)
        return carry

    lax.fori_loop(0, 2 * half_tiles + 1, clear, 0, unroll=8)

    def pair(table, e0, e1, cuts):
        one = table[(e0 >> 1) + tiles * (e0 & 1)]
        two = table[(e1 >> 1) + tiles * (1 - (e1 & 1))]
        return jnp.concatenate(
            [one[r : r + 16] * mlo + two[r : r + 16] * mhi for r in range(0, cuts, 16)], axis=0
        )

    def first(group, buffer):
        squares = []
        for j in range(ITEMS):
            v = slots[group * ITEMS + j]
            t = v >> 2
            at = t * 12 + (v & 3) * 4
            e = [near[at + k] for k in range(4)]
            source = jnp.concatenate(
                [pair(feats, e[0], e[1], 48), pair(feats, e[2], e[3], 48)], axis=1
            )
            weights[buffer, j] = jnp.concatenate(
                [pair(wz, e[0], e[1], 16), pair(wz, e[2], e[3], 16)], axis=1
            )
            squares.append(dot(tt[pl.ds(pl.multiple_of(t * 64, 64), 64), :], source))
        for j, square in enumerate(squares):
            kernels[buffer, j] = lax.rsqrt(square).astype(BF16)

    def second(group, buffer):
        values = [dot_t(weights[buffer, j], kernels[buffer, j]) for j in range(ITEMS)]
        for j, value in enumerate(values):
            acc[slots[group * ITEMS + j] >> 2] += value

    first(0, 0)

    def items(i, carry):
        first(2 * i + 1, 1)
        second(2 * i, 0)
        first(2 * i + 2, 0)
        second(2 * i + 1, 1)
        return carry

    lax.fori_loop(0, slots[slots.shape[0] - 1], items, 0)

    def join(v, carry):
        near_out[v] = jnp.concatenate([acc[2 * v], acc[2 * v + 1]], axis=1)
        return carry

    lax.fori_loop(0, half_tiles, join, 0, unroll=4)

    done = [pltpu.make_async_copy(near_out, near_hbm, out_sems.at[0])]
    done[0].start()
    for copy in copies[6:]:
        copy.wait()
    low16 = low_half((16, 128))
    for base, pay in ((own_boxes, extra_below), (2 * own_boxes, extra_above)):

        def ghost_box(i, carry, base=base, pay=pay):
            pair = pay[16 + i].astype(F32)
            turned = roll_half(pair)
            ab[base + 2 * i] = jnp.where(low16, pair, turned).astype(BF16)
            ab[base + 2 * i + 1] = jnp.where(low16, turned, pair).astype(BF16)
            return carry

        lax.fori_loop(0, own_boxes // 2, ghost_box, 0, unroll=4)

    def couple(b, carry):
        total = None
        for kg in range(2):
            rows = []
            for k in range(8):
                source = ab[box_list[b * 16 + kg * 8 + k]]
                rows += [source * mlo, source * mhi]
            at = pl.ds(pl.multiple_of((b * 2 + kg) * 256, 256), 256)
            wide = dot_t(jnp.concatenate(rows, axis=0), coup[at, :])
            part = pick_slots([wide[s * 32 : s * 32 + 32] for s in range(8)])
            total = part if total is None else total + part
        fields[b] = total
        return carry

    lax.fori_loop(0, fields.shape[0], couple, 0, unroll=2)
    done.append(pltpu.make_async_copy(fields, fields_hbm, out_sems.at[1]))
    done[1].start()
    for copy in done:
        copy.wait()


def fold(parts, unfold):
    rows = [jnp.concatenate([p[:16], p[16:]], axis=1) for p in parts]
    high = [r.astype(BF16) for r in rows]
    low = [(r - h.astype(F32)).astype(BF16) for r, h in zip(rows, high)]
    out = dot(jnp.concatenate(high + low, axis=0), unfold[...])
    n = 16 * len(parts)
    return out[:n] + out[n:]


def down_kernel(
    where,
    root_list,
    roots_in,
    rcoup_in,
    rtrans_in,
    fields_in,
    trans_in,
    basis_in,
    near_in,
    unfold_in,
    back_in,
    out_hbm,
    roots,
    rcoup,
    rtrans,
    fields,
    trans,
    basis,
    near,
    unfold,
    back,
    out,
    bf,
    far_high,
    far_low,
    sems,
    out_sem,
):
    def half_of(ref, rows):
        return ref.at[pl.ds(pl.multiple_of(where[0] * rows, rows), rows)]

    copies = copied(
        (
            (roots_in, roots),
            (rcoup_in, rcoup),
            (unfold_in, unfold),
            (half_of(rtrans_in, rtrans.shape[0]), rtrans),
            (fields_in, fields),
            (half_of(trans_in, trans.shape[0]), trans),
            (half_of(basis_in, basis.shape[0]), basis),
            (back_in, back),
            (near_in, near),
        ),
        sems,
    )
    for copy in copies[:3]:
        copy.wait()
    mlo, mhi = half_masks()
    low8 = low_half((8, 128))
    half_boxes = fields.shape[0]

    total = None
    for kg in range(2):
        rows = []
        for k in range(8):
            if kg * 8 + k < 12:
                source = roots[root_list[kg * 8 + k]].astype(F32)
                turned = roll_half(source)
                even = jnp.concatenate([source, turned], axis=0).astype(BF16) * mlo
                odd = jnp.concatenate([turned, source], axis=0).astype(BF16) * mhi
                rows += [even, odd]
            else:
                rows.append(jnp.zeros((32, 128), BF16))
        wide = dot_t(jnp.concatenate(rows, axis=0), rcoup[kg * 256 : kg * 256 + 256, :])
        part = pick_slots([wide[s * 32 : s * 32 + 32] for s in range(8)])
        total = part if total is None else total + part
    rf = fold([total], unfold).astype(BF16)
    moving = jnp.concatenate([rf * mlo, rf * mhi], axis=0)
    slot = lane_slot((32, 256))
    for copy in copies[3:5]:
        copy.wait()
    for g in range(half_boxes // 8):
        pushed = dot_t(moving, rtrans[g * 256 : g * 256 + 256, :])
        sums = [fields[g * 8 + s] + jnp.where(slot == s, pushed, 0.0) for s in range(8)]
        bf[g * 128 : g * 128 + 128, :] = fold(sums, unfold).astype(BF16)

    masks = slot_masks(16)
    for copy in copies[5:7]:
        copy.wait()

    def leaves(i, carry):
        picks = [i * DOWN + j for j in range(DOWN)]
        rows = [pl.ds(pl.multiple_of(b * 256, 256), 256) for b in picks]
        spots = [pl.ds(pl.multiple_of(b * 16, 16), 16) for b in picks]
        hs = []
        for r, at in zip(rows, spots):
            field = bf[at, :]
            moving = jnp.concatenate([field * mlo, field * mhi], axis=0)
            hs.append(dot_t(moving, trans[r, :]).astype(BF16))
        wides = [
            jnp.concatenate(
                [jnp.concatenate([h[:16] * m, h[16:] * m], axis=1) for m in masks], axis=0
            )
            for h in hs
        ]
        lfs = [dot(wide, unfold[...]).astype(BF16) for wide in wides]
        fars = []
        for lf, r in zip(lfs, rows):
            parts = []
            for s in range(8):
                one = lf[s * 16 : s * 16 + 16]
                parts += [one * mlo, one * mhi]
            fars.append(dot_t(jnp.concatenate(parts, axis=0), basis[r, :]))
        for far, at in zip(fars, spots):
            far = pick_slots([far[s * 32 : s * 32 + 32] for s in range(8)])
            far = jnp.concatenate([far[:16], far[16:]], axis=1)
            high = far.astype(BF16)
            far_high[at, :] = high
            far_low[at, :] = (far - high.astype(F32)).astype(BF16)
        return carry

    lax.fori_loop(0, half_boxes // DOWN, leaves, 0)

    for copy in copies[7:]:
        copy.wait()

    def emit(i, carry):
        at = pl.ds(pl.multiple_of(i * 64, 64), 64)
        far = dot(far_high[at, :], back[...]) + dot(far_low[at, :], back[...])
        for b in range(4):
            for j in range(4):
                v = (i * 4 + b) * 4 + j
                value = far[b * 16 : b * 16 + 16, j * 128 : j * 128 + 128] + near[v]
                out[:, pl.ds(pl.multiple_of(v * 128, 128), 128)] = value.astype(BF16)
        return carry

    lax.fori_loop(0, half_boxes // 4, emit, 0)
    last = pltpu.make_async_copy(out, out_hbm, out_sem)
    last.start()
    last.wait()


def natural(matrices):
    n = matrices.shape[0]
    return jnp.transpose(matrices.reshape(n // 8, 8, 32, 128), (0, 2, 1, 3)).reshape(n * 32, 128)


def whole(shape=None):
    return pl.BlockSpec(memory_space=VMEM)


def smem():
    return pl.BlockSpec(memory_space=pltpu.SMEM)


def shape_of(shape, dtype):
    return jax.ShapeDtypeStruct(shape, dtype)


def hbm():
    return pl.BlockSpec(memory_space=pltpu.HBM)


def params():
    return pltpu.CompilerParams(vmem_limit_bytes=60 * 1024 * 1024)


def shifted(value, by):
    peers = lax.axis_size("leaf")
    pairs = [(i, i + by) for i in range(peers) if 0 <= i + by < peers]
    return lax.ppermute(value, "leaf", pairs)


def gather_roots(root):
    peers = lax.axis_size("leaf")
    copies = jnp.broadcast_to(root[None], (peers,) + root.shape)
    return lax.all_to_all(copies, "leaf", 0, 0, tiled=True)


def per_device(
    density,
    coords,
    qweight,
    leaf_basis,
    box_transfer,
    root_transfer,
    box_coupling,
    root_coupling,
    near_list,
    near_count,
    box_list,
    root_list,
    ghost_send,
):
    points = density.shape[1]
    tiles = points // 128
    box_count = tiles // 4
    half_leaves = near_list.shape[0]
    half_boxes = box_list.shape[0]
    where = lax.axis_index("sub").astype(jnp.int32).reshape(1)
    basis = natural(leaf_basis)
    trans = natural(box_transfer)
    rtrans = natural(root_transfer)
    coup = natural(box_coupling.reshape(half_boxes * 16, 4096))
    rcoup = natural(jnp.pad(root_coupling[0], ((0, 4), (0, 0))))
    order = jnp.asarray(in_order_matrix(), BF16)
    back = jnp.asarray(in_order_matrix().T.copy(), BF16)
    spread_m = jnp.asarray(spread_matrix(), BF16)
    unfold = jnp.asarray(unfold_matrix(), BF16)

    zw, pay_low, pay_high, boxes, root = pl.pallas_call(
        up_kernel,
        name="up",
        out_shape=(
            shape_of((tiles, 16, 128), BF16),
            shape_of((64, 16, 128), BF16),
            shape_of((64, 16, 128), BF16),
            shape_of((box_count, 16, 128), BF16),
            shape_of((8, 128), BF16),
        ),
        in_specs=[smem()] + [hbm()] * 8,
        out_specs=tuple([hbm()] * 5),
        scratch_shapes=[
            VMEM(density.shape, BF16),
            VMEM((1, points), F32),
            VMEM(coords.shape, F32),
            VMEM(basis.shape, BF16),
            VMEM(trans.shape, BF16),
            VMEM(rtrans.shape, BF16),
            VMEM(order.shape, BF16),
            VMEM(spread_m.shape, BF16),
            VMEM((box_count * 16, 512), BF16),
            VMEM((box_count * 16, 512), BF16),
            VMEM((2 * tiles, 8, 128), F32),
            VMEM((2 * tiles, 16, 128), BF16),
            VMEM((64, 16, 128), BF16),
            VMEM((64, 16, 128), BF16),
            VMEM((box_count, 16, 128), BF16),
            VMEM((8, 128), BF16),
            pltpu.SemaphoreType.DMA((8,)),
            pltpu.SemaphoreType.DMA((5,)),
        ],
        compiler_params=params(),
    )(
        ghost_send.reshape(-1),
        density,
        qweight.reshape(1, points),
        coords,
        basis,
        trans,
        rtrans,
        order,
        spread_m,
    )
    pay_below = shifted(pay_low, 1)
    pay_above = shifted(pay_high, -1)
    roots = gather_roots(root)

    live = lax.broadcasted_iota(jnp.int32, near_list.shape, 1) < near_count[:, None]
    entries = jnp.where(live, near_list, 2 * tiles + 128)
    entries = jnp.pad(entries, ((0, 1), (0, 0)), constant_values=2 * tiles + 128).reshape(-1)
    fours = (near_count + 3) // 4
    index = jnp.arange(half_leaves, dtype=jnp.int32)
    ends = jnp.sum(jnp.where(index[None, :] <= index[:, None], fours[None, :], 0), axis=1)
    slot = jnp.arange(half_leaves * 3 + 3 * ITEMS, dtype=jnp.int32)
    passed = ends[None, :] <= slot[:, None]
    target = jnp.sum(passed.astype(jnp.int32), axis=1)
    begin = jnp.max(jnp.where(passed, ends[None, :], 0), axis=1)
    slots = jnp.where(target < half_leaves, target * 4 + slot - begin, half_leaves * 4)
    rounds = ((ends[-1:] + 2 * ITEMS - 1) // (2 * ITEMS)).astype(jnp.int32)

    slots = jnp.concatenate([slots, rounds])

    table = 2 * (tiles + 65)
    near, fields = pl.pallas_call(
        near_kernel,
        name="near",
        out_shape=(
            shape_of((half_leaves // 2, 16, 128), F32),
            shape_of((half_boxes, 32, 256), F32),
        ),
        in_specs=[smem()] * 4 + [hbm()] * 6,
        out_specs=(hbm(), hbm()),
        scratch_shapes=[
            VMEM(coords.shape, F32),
            VMEM((32, 16, 128), BF16),
            VMEM((32, 16, 128), BF16),
            VMEM(coup.shape, BF16),
            VMEM((half_leaves // 2, 16, 128), F32),
            VMEM((half_boxes, 32, 256), F32),
            VMEM((table, 48, 128), BF16),
            VMEM((table, 16, 128), BF16),
            VMEM(((half_leaves + 1) * 64, 48), BF16),
            VMEM((half_leaves + 1, 16, 64), F32),
            VMEM((3 * box_count, 16, 128), BF16),
            VMEM((2, ITEMS, 64, 256), BF16),
            VMEM((2, ITEMS, 16, 256), BF16),
            pltpu.SemaphoreType.DMA((8,)),
            pltpu.SemaphoreType.DMA((2,)),
        ],
        compiler_params=params(),
        cost_estimate=pl.CostEstimate(flops=10**9, bytes_accessed=10**7, transcendentals=6 * 10**6),
    )(
        where,
        entries,
        slots,
        box_list.reshape(-1),
        zw,
        coords,
        pay_below,
        pay_above,
        boxes,
        coup,
    )

    return pl.pallas_call(
        down_kernel,
        name="down",
        out_shape=shape_of((16, half_leaves * 64), BF16),
        in_specs=[smem()] * 2 + [hbm()] * 9,
        out_specs=hbm(),
        scratch_shapes=[
            VMEM(roots.shape, BF16),
            VMEM(rcoup.shape, BF16),
            VMEM((half_boxes * 32, 128), BF16),
            VMEM(fields.shape, F32),
            VMEM((half_leaves * 32, 128), BF16),
            VMEM((half_leaves * 32, 128), BF16),
            VMEM(near.shape, F32),
            VMEM(unfold.shape, BF16),
            VMEM(back.shape, BF16),
            VMEM((16, half_leaves * 64), BF16),
            VMEM((half_boxes * 16, 128), BF16),
            VMEM((half_boxes * 16, 512), BF16),
            VMEM((half_boxes * 16, 512), BF16),
            pltpu.SemaphoreType.DMA((9,)),
            pltpu.SemaphoreType.DMA,
        ],
        compiler_params=params(),
    )(where, root_list.reshape(-1), roots, rcoup, rtrans, fields, trans, basis, near, unfold, back)


def solution(mesh):
    in_specs = (
        P(None, "leaf"),
        P(None, "leaf"),
        P("leaf"),
        P("leaf", None),
        P("leaf", None),
        P("leaf", None),
        P(("leaf", "sub"), None, None),
        P("leaf", None, None),
        P(("leaf", "sub"), None),
        P(("leaf", "sub")),
        P(("leaf", "sub"), None),
        P("leaf", None),
        P("leaf", "sub", None, None),
    )
    out_specs = P(None, ("leaf", "sub"))
    return jax.shard_map(
        per_device, mesh=mesh, in_specs=in_specs, out_specs=out_specs, check_vma=False
    )
```

```python
import functools

import jax
import jax.numpy as jnp
import numpy as np
from jax import lax
from jax.experimental import pallas as pl
from jax.experimental.pallas import tpu as pltpu
from jax.sharding import PartitionSpec as P

LEAF = 64
RANK = 64
DELTA_SQ = 0.0025
UP = 8
ITEMS = 16
DOWN = 8
F32 = jnp.float32
BF16 = jnp.bfloat16
VMEM = pltpu.VMEM
NT = (((1,), (1,)), ((), ()))


def in_order_matrix():
    out = np.zeros((512, 512), np.float32)
    for leaf in range(8):
        for m in range(32):
            for par in range(2):
                out[leaf * 64 + 2 * m + par, par * 256 + m * 8 + leaf] = 1
    return out


def unfold_matrix():
    out = np.zeros((512, 128), np.float32)
    for par in range(2):
        for m in range(32):
            for leaf in range(8):
                out[par * 256 + m * 8 + leaf, 2 * m + par] = 1
                out[par * 256 + m * 8 + leaf, 64 + 2 * m + par] = 1
    return out


def spread_matrix():
    out = unfold_matrix().T.copy()
    out[64:] = 0
    return out


def dot(a, b):
    return jnp.dot(a, b, preferred_element_type=F32)


def dot_t(a, b):
    return lax.dot_general(a, b, NT, preferred_element_type=F32)


def low_half(shape):
    return lax.broadcasted_iota(jnp.int32, shape, len(shape) - 1) < 64


def lane_slot(shape):
    return lax.broadcasted_iota(jnp.int32, shape, len(shape) - 1) & 7


def roll_half(value):
    return pltpu.roll(value, 64, value.ndim - 1)


def half_masks():
    low = low_half((16, 128))
    return (
        jnp.where(low, 1.0, 0.0).astype(BF16),
        jnp.where(low, 0.0, 1.0).astype(BF16),
    )


def slot_masks(rows):
    slot = lane_slot((rows, 256))
    return [jnp.where(slot == s, 1.0, 0.0).astype(BF16) for s in range(8)]


def pick_slots(parts):
    slot = lane_slot(parts[0].shape)
    out = parts[0]
    for s in range(1, 8):
        out = jnp.where(slot == s, parts[s], out)
    return out


def add_halves(value):
    chosen = jnp.where(low_half((16, 128)), value[:16], value[16:])
    return chosen + roll_half(chosen)


def gathered(wide):
    picked = pick_slots([wide[s * 16 : s * 16 + 16] for s in range(8)]).astype(BF16)
    return jnp.concatenate([picked[:, :256], picked[:, 256:]], axis=0)


def copied(pairs, sems):
    copies = [pltpu.make_async_copy(a, b, sems.at[i]) for i, (a, b) in enumerate(pairs)]
    for copy in copies:
        copy.start()
    return copies


def up_kernel(
    send,
    dens_in,
    qw_in,
    coords_in,
    basis_in,
    trans_in,
    order_in,
    spread_in,
    zw_out,
    pay_low_out,
    pay_high_out,
    boxes_out,
    dens,
    qw,
    coords,
    basis,
    trans,
    order,
    spread_ref,
    flat,
    ordered,
    cz,
    rolled,
    pay_low,
    pay_high,
    boxes,
    sems,
    out_sems,
):
    sources = (dens_in, qw_in, coords_in, order_in, basis_in, spread_in, trans_in)
    places = (dens, qw, coords, order, basis, spread_ref, trans)
    copies = copied(zip(sources, places), sems)
    for copy in copies[:3]:
        copy.wait()
    tiles = dens.shape[1] // 128
    box_count = tiles // 4
    mlo, mhi = half_masks()

    def weigh(b, carry):
        at = pl.multiple_of(b * 512, 512)
        row = pl.multiple_of(b * 16, 16)
        w = (dens[:, pl.ds(at, 512)].astype(F32) * qw[:, pl.ds(at, 512)]).astype(BF16)
        flat[pl.ds(row, 16), :] = w
        wide = w.astype(F32)
        c = coords[:, pl.ds(at, 512)]
        c = jnp.concatenate([c, jnp.zeros((5, 512), F32)], axis=0)
        for j in range(4):
            v = b * 4 + j
            cut = slice(j * 128, j * 128 + 128)
            rolled[2 * v] = w[:, cut]
            rolled[2 * v + 1] = roll_half(wide[:, cut]).astype(BF16)
            cz[2 * v] = c[:, cut]
            cz[2 * v + 1] = roll_half(c[:, cut])
        return carry

    lax.fori_loop(0, box_count, weigh, 0, unroll=8)

    kept = pltpu.make_async_copy(rolled, zw_out, out_sems.at[0])
    kept.start()
    copies[3].wait()
    ordered[...] = dot(flat[...], order[...]).astype(BF16)

    low8 = low_half((8, 128))

    def pack(i, carry):
        for d, pay in ((0, pay_low), (1, pay_high)):
            parts = []
            for j in range(2):
                pair = i * 2 + j
                s0 = send[0, 0, d, pair * 2]
                s1 = send[0, 0, d, pair * 2 + 1]
                i0 = s0
                i1 = s1 ^ 1
                pay[pair] = rolled[i0] * mlo + rolled[i1] * mhi
                c = jnp.where(low8, cz[i0], cz[i1])
                high = c.astype(BF16).astype(F32)
                parts += [high[0:4], (c - high)[0:4]]
            pay[32 + i] = jnp.concatenate(parts, axis=0).astype(BF16)
        return carry

    lax.fori_loop(0, 16, pack, 0, unroll=8)

    masks = slot_masks(32)

    for copy in copies[4:]:
        copy.wait()

    def up(i, carry):
        picks = [i * UP + j for j in range(UP)]
        rows = [pl.ds(pl.multiple_of(b * 256, 256), 256) for b in picks]
        outs = []
        for b, r in zip(picks, rows):
            w = ordered[pl.ds(pl.multiple_of(b * 16, 16), 16), :]
            w = jnp.concatenate([w[:, :256], w[:, 256:]], axis=0)
            moving = jnp.concatenate([w * m for m in masks], axis=0)
            outs.append(dot(moving, basis[r, :]))
        coefs = [
            jnp.concatenate(
                [add_halves(out[s * 32 : s * 32 + 32]) for s in range(8)], axis=0
            ).astype(BF16)
            for out in outs
        ]
        wides = [dot(c, spread_ref[...]) for c in coefs]
        lifted = [dot(gathered(w), trans[r, :]) for w, r in zip(wides, rows)]
        for b, total in zip(picks, lifted):
            boxes[b] = add_halves(total).astype(BF16)
        return carry

    lax.fori_loop(0, box_count // UP, up, 0)

    def finish(i, carry):
        pair = boxes[2 * i] * mlo + boxes[2 * i + 1] * mhi
        pay_low[48 + i] = pair
        pay_high[48 + i] = pair
        return carry

    lax.fori_loop(0, box_count // 2, finish, 0, unroll=4)

    sends = [
        pltpu.make_async_copy(a, b, out_sems.at[i])
        for i, (a, b) in ((1, (pay_low, pay_low_out)), (2, (pay_high, pay_high_out)), (3, (boxes, boxes_out)))
    ]
    for copy in sends:
        copy.start()
    for copy in sends + [kept]:
        copy.wait()


def top_kernel(boxes_in, rtrans_in, spread_in, root_out, boxes, rtrans, spread_ref, root, sems):
    copies = copied(
        ((boxes_in, boxes), (spread_in, spread_ref), (rtrans_in, rtrans)), sems
    )
    for copy in copies[:2]:
        copy.wait()
    groups = boxes.shape[0] // 8
    wides = [
        dot(jnp.concatenate([boxes[g * 8 + s] for s in range(8)], axis=0), spread_ref[...])
        for g in range(groups)
    ]
    copies[2].wait()
    total = jnp.zeros((32, 128), F32)
    for g, wide in enumerate(wides):
        total += dot(gathered(wide), rtrans[g * 256 : g * 256 + 256, :])
    total = add_halves(total)
    total = jnp.where(low_half((8, 128)), total[:8], total[8:]).astype(BF16)

    def copy_root(i, carry):
        root[i] = total
        return carry

    lax.fori_loop(0, root.shape[0], copy_root, 0, unroll=16)
    last = pltpu.make_async_copy(root, root_out, sems.at[3])
    last.start()
    last.wait()


def split3(value):
    high = value.astype(BF16).astype(F32)
    rest = value - high
    mid = rest.astype(BF16).astype(F32)
    return high, mid, rest - mid


def near_kernel(
    near,
    count,
    box_list,
    zw,
    coords_in,
    pay_below,
    pay_above,
    boxes,
    coup_in,
    near_hbm,
    fields_hbm,
    coords,
    extra_below,
    extra_above,
    coup,
    near_out,
    fields,
    feats,
    wz,
    tt,
    acc,
    ab,
    kernels,
    weights,
    live_masks,
    slots,
    sems,
    out_sems,
):
    half_leaves = count.shape[0]
    own_tiles = zw.shape[0] // 2
    ghost = 32
    half_tiles = own_tiles // 2
    mlo, mhi = half_masks()
    own_boxes = boxes.shape[0]
    copies = copied(
        (
            (coords_in, coords),
            (zw, wz.at[pl.ds(0, 2 * own_tiles)]),
            (pay_below, extra_below),
            (pay_above, extra_above),
            (boxes, ab.at[pl.ds(0, own_boxes)]),
            (coup_in, coup),
        ),
        sems,
    )

    def listing(t, listed):
        for k in range(3):
            slots[listed + k] = t * 516 + k
        return listed + ((count[t] + 3) >> 2)

    listed = lax.fori_loop(0, half_leaves, listing, 0, unroll=8)
    for k in range(3 * ITEMS):
        slots[listed + k] = half_leaves * 512
    rounds = (listed + 2 * ITEMS - 1) // (2 * ITEMS)

    def clear(i, carry):
        acc[i] = jnp.zeros((16, 64), F32)
        return carry

    lax.fori_loop(0, 2 * half_tiles + 1, clear, 0, unroll=8)

    for n in range(13):
        for k in range(4):
            part = (mlo, mhi)[k % 2]
            live_masks[n * 4 + k] = part if k < n else jnp.zeros_like(part)

    def source_pair(e0, e1):
        one = feats[e0]
        two = feats[e1 ^ 1]
        return jnp.concatenate(
            [one[r : r + 16] * mlo + two[r : r + 16] * mhi for r in range(0, 48, 16)], axis=0
        )

    def weight_pair(e0, e1, at):
        return wz[e0] * live_masks[at] + wz[e1 ^ 1] * live_masks[at + 1]

    def first(group, buffer):
        squares = []
        for j in range(ITEMS):
            v = slots[group * ITEMS + j]
            t = (v >> 2) & (half_leaves - 1)
            at = (v & 3) * 4
            live = (count[t] - at) * 4
            e = [near[at + k, t] for k in range(4)]
            source = jnp.concatenate([source_pair(e[0], e[1]), source_pair(e[2], e[3])], axis=1)
            weights[buffer, j] = jnp.concatenate(
                [weight_pair(e[0], e[1], live), weight_pair(e[2], e[3], live + 2)], axis=1
            )
            squares.append(dot(tt[pl.ds(pl.multiple_of(t * 64, 64), 64), :], source))
        for j, square in enumerate(squares):
            kernels[buffer, j] = lax.rsqrt(square).astype(BF16)

    def second(group, buffer):
        values = [dot_t(weights[buffer, j], kernels[buffer, j]) for j in range(ITEMS)]
        for j, value in enumerate(values):
            acc[slots[group * ITEMS + j] >> 9] += value

    copies[0].wait()
    row8 = lax.broadcasted_iota(jnp.int32, (8, 128), 0)

    def put_source(v, c):
        c = jnp.where(row8 < 3, c - 0.5, 0.0)
        size = jnp.sum(c * c, axis=0, keepdims=True)
        u = jnp.where(row8 < 3, c, jnp.where(row8 == 3, size, jnp.where(row8 == 4, 1.0, 0.0)))
        for at, block in ((2 * v, u), (2 * v + 1, roll_half(u))):
            h, m, l = split3(block)
            feats[at] = jnp.concatenate([h, m, l, h, m, h], axis=0).astype(BF16)

    def own(i, carry):
        for j in range(16):
            v = i * 16 + j
            c = coords[:, pl.ds(pl.multiple_of(v * 128, 128), 128)]
            c = jnp.concatenate([c, jnp.zeros((5, 128), F32)], axis=0)
            put_source(v, c)
        return carry

    lax.fori_loop(0, own_tiles // 16, own, 0)
    eye = jnp.where(
        lax.broadcasted_iota(jnp.int32, (128, 128), 0)
        == lax.broadcasted_iota(jnp.int32, (128, 128), 1),
        1.0,
        0.0,
    ).astype(BF16)
    first_tile = lax.axis_index("sub") * half_tiles

    def target(i, carry):
        blocks = []
        for j in range(16):
            v = i * 16 + j
            c = coords[:, pl.ds(pl.multiple_of((first_tile + v) * 128, 128), 128)]
            c = jnp.concatenate([c, jnp.zeros((5, 128), F32)], axis=0)
            c = jnp.where(row8 < 3, c - 0.5, 0.0)
            size = jnp.sum(c * c, axis=0, keepdims=True) + DELTA_SQ
            u = jnp.where(
                row8 < 3, -2.0 * c, jnp.where(row8 == 3, 1.0, jnp.where(row8 == 4, size, 0.0))
            )
            h, m, l = split3(u)
            blocks.append(jnp.concatenate([h, h, h, m, m, l], axis=0).astype(BF16))
        for j, turned in enumerate([dot_t(eye, block) for block in blocks]):
            tt[pl.ds(pl.multiple_of((i * 16 + j) * 128, 128), 128), :] = turned.astype(BF16)
        return carry

    lax.fori_loop(0, half_tiles // 16, target, 0)

    for copy in copies[1:4]:
        copy.wait()
    for base, pay in ((own_tiles, extra_below), (own_tiles + ghost, extra_above)):

        def ghosts(i, carry, base=base, pay=pay):
            both = pay[32 + i].astype(F32)
            for j in range(2):
                v = i * 2 + j
                c = both[j * 8 : j * 8 + 4] + both[j * 8 + 4 : j * 8 + 8]
                c = jnp.concatenate([c, jnp.zeros((4, 128), F32)], axis=0)
                put_source(base + v, c)
                wz[2 * (base + v)] = pay[v]
                wz[2 * (base + v) + 1] = roll_half(pay[v].astype(F32)).astype(BF16)
            return carry

        lax.fori_loop(0, ghost // 2, ghosts, 0, unroll=8)

    for copy in copies[4:]:
        copy.wait()
    low16 = low_half((16, 128))
    for base, pay in ((own_boxes, extra_below), (2 * own_boxes, extra_above)):

        def ghost_box(i, carry, base=base, pay=pay):
            pair = pay[48 + i].astype(F32)
            turned = roll_half(pair)
            ab[base + 2 * i] = jnp.where(low16, pair, turned).astype(BF16)
            ab[base + 2 * i + 1] = jnp.where(low16, turned, pair).astype(BF16)
            return carry

        lax.fori_loop(0, own_boxes // 2, ghost_box, 0, unroll=16)

    def couple(b, carry):
        total = None
        for kg in range(2):
            rows = []
            for k in range(8):
                source = ab[box_list[b, kg * 8 + k]]
                rows += [source * mlo, source * mhi]
            at = pl.ds(pl.multiple_of((b * 2 + kg) * 256, 256), 256)
            wide = dot_t(jnp.concatenate(rows, axis=0), coup[at, :])
            part = pick_slots([wide[s * 32 : s * 32 + 32] for s in range(8)])
            total = part if total is None else total + part
        fields[b] = total
        return carry

    lax.fori_loop(0, fields.shape[0], couple, 0, unroll=8)
    coupled = pltpu.make_async_copy(fields, fields_hbm, out_sems.at[1])
    coupled.start()

    first(0, 0)

    def items(i, carry):
        first(2 * i + 1, 1)
        second(2 * i, 0)
        first(2 * i + 2, 0)
        second(2 * i + 1, 1)
        return carry

    lax.fori_loop(0, rounds, items, 0)

    def join(v, carry):
        near_out[v] = jnp.concatenate([acc[2 * v], acc[2 * v + 1]], axis=1)
        return carry

    lax.fori_loop(0, half_tiles, join, 0, unroll=16)

    last = pltpu.make_async_copy(near_out, near_hbm, out_sems.at[0])
    last.start()
    coupled.wait()
    last.wait()


def fold(parts, unfold):
    rows = [jnp.concatenate([p[:16], p[16:]], axis=1) for p in parts]
    high = [r.astype(BF16) for r in rows]
    low = [(r - h.astype(F32)).astype(BF16) for r, h in zip(rows, high)]
    out = dot(jnp.concatenate(high + low, axis=0), unfold[...])
    n = 16 * len(parts)
    return out[:n] + out[n:]


def down_kernel(
    root_list,
    roots_in,
    rcoup_in,
    rtrans_in,
    fields_in,
    trans_in,
    basis_in,
    near_in,
    unfold_in,
    back_in,
    out_hbm,
    roots,
    rcoup,
    rtrans,
    fields,
    trans,
    basis,
    near,
    unfold,
    back,
    out,
    bf,
    far_high,
    far_low,
    sems,
    out_sem,
):
    def half_of(ref, rows):
        return ref.at[pl.ds(pl.multiple_of(lax.axis_index("sub") * rows, rows), rows)]

    copies = copied(
        (
            (roots_in, roots),
            (rcoup_in, rcoup),
            (unfold_in, unfold),
            (half_of(rtrans_in, rtrans.shape[0]), rtrans),
            (fields_in, fields),
            (half_of(trans_in, trans.shape[0]), trans),
            (half_of(basis_in, basis.shape[0]), basis),
            (back_in, back),
            (near_in, near),
        ),
        sems,
    )
    for copy in copies[:3]:
        copy.wait()
    mlo, mhi = half_masks()
    low8 = low_half((8, 128))
    half_boxes = fields.shape[0]

    total = None
    known = rcoup.shape[0]
    for kg in range(2):
        rows = []
        have = min(known - kg * 8, 8)
        blocks = []
        for m in range(32):
            block = rcoup[:, m * 128 : m * 128 + 128].astype(F32)[kg * 8 : kg * 8 + have]
            if have < 8:
                block = jnp.concatenate([block, jnp.zeros((8 - have, 128), F32)], axis=0)
            blocks.append(block)
        matrix = jnp.concatenate(blocks, axis=0).astype(BF16)
        for k in range(8):
            if kg * 8 + k < known:
                source = roots[root_list[0, kg * 8 + k]].astype(F32)
                turned = roll_half(source)
                even = jnp.concatenate([source, turned], axis=0).astype(BF16) * mlo
                odd = jnp.concatenate([turned, source], axis=0).astype(BF16) * mhi
                rows += [even, odd]
            else:
                rows.append(jnp.zeros((32, 128), BF16))
        wide = dot_t(jnp.concatenate(rows, axis=0), matrix)
        part = pick_slots([wide[s * 32 : s * 32 + 32] for s in range(8)])
        total = part if total is None else total + part
    rf = fold([total], unfold).astype(BF16)
    moving = jnp.concatenate([rf * mlo, rf * mhi], axis=0)
    slot = lane_slot((32, 256))
    for copy in copies[3:5]:
        copy.wait()
    for g in range(half_boxes // 8):
        pushed = dot_t(moving, rtrans[g * 256 : g * 256 + 256, :])
        sums = [fields[g * 8 + s] + jnp.where(slot == s, pushed, 0.0) for s in range(8)]
        bf[g * 128 : g * 128 + 128, :] = fold(sums, unfold).astype(BF16)

    masks = slot_masks(16)
    for copy in copies[5:7]:
        copy.wait()

    def leaves(i, carry):
        picks = [i * DOWN + j for j in range(DOWN)]
        rows = [pl.ds(pl.multiple_of(b * 256, 256), 256) for b in picks]
        spots = [pl.ds(pl.multiple_of(b * 16, 16), 16) for b in picks]
        hs = []
        for r, at in zip(rows, spots):
            field = bf[at, :]
            moving = jnp.concatenate([field * mlo, field * mhi], axis=0)
            hs.append(dot_t(moving, trans[r, :]).astype(BF16))
        wides = [
            jnp.concatenate(
                [jnp.concatenate([h[:16] * m, h[16:] * m], axis=1) for m in masks], axis=0
            )
            for h in hs
        ]
        lfs = [dot(wide, unfold[...]).astype(BF16) for wide in wides]
        fars = []
        for lf, r in zip(lfs, rows):
            parts = []
            for s in range(8):
                one = lf[s * 16 : s * 16 + 16]
                parts += [one * mlo, one * mhi]
            fars.append(dot_t(jnp.concatenate(parts, axis=0), basis[r, :]))
        for far, at in zip(fars, spots):
            far = pick_slots([far[s * 32 : s * 32 + 32] for s in range(8)])
            far = jnp.concatenate([far[:16], far[16:]], axis=1)
            high = far.astype(BF16)
            far_high[at, :] = high
            far_low[at, :] = (far - high.astype(F32)).astype(BF16)
        return carry

    lax.fori_loop(0, half_boxes // DOWN, leaves, 0)

    for copy in copies[7:]:
        copy.wait()

    def emit(i, carry):
        at = pl.ds(pl.multiple_of(i * 64, 64), 64)
        far = dot(far_high[at, :], back[...]) + dot(far_low[at, :], back[...])
        for b in range(4):
            for j in range(4):
                v = (i * 4 + b) * 4 + j
                value = far[b * 16 : b * 16 + 16, j * 128 : j * 128 + 128] + near[v]
                out[:, pl.ds(pl.multiple_of(v * 128, 128), 128)] = value.astype(BF16)
        return carry

    lax.fori_loop(0, half_boxes // 4, emit, 0)
    last = pltpu.make_async_copy(out, out_hbm, out_sem)
    last.start()
    last.wait()


def natural(matrices):
    n = matrices.shape[0]
    return jnp.transpose(matrices.reshape(n // 8, 8, 32, 128), (0, 2, 1, 3)).reshape(n * 32, 128)


def whole(shape=None):
    return pl.BlockSpec(memory_space=VMEM)


def smem():
    return pl.BlockSpec(memory_space=pltpu.SMEM)


def shape_of(shape, dtype):
    return jax.ShapeDtypeStruct(shape, dtype)


def hbm():
    return pl.BlockSpec(memory_space=pltpu.HBM)


def params():
    return pltpu.CompilerParams(vmem_limit_bytes=66_900_000)


def shifted(value, by):
    peers = lax.axis_size("leaf")
    pairs = [(i, i + by) for i in range(peers) if 0 <= i + by < peers]
    return lax.ppermute(value, "leaf", pairs)


def per_device(
    density,
    coords,
    qweight,
    leaf_basis,
    box_transfer,
    root_transfer,
    box_coupling,
    root_coupling,
    near_list,
    near_count,
    box_list,
    root_list,
    ghost_send,
):
    points = density.shape[1]
    peers = lax.axis_size("leaf")
    tiles = points // 128
    box_count = tiles // 4
    half_leaves = near_list.shape[0]
    half_boxes = box_list.shape[0]
    basis = natural(leaf_basis)
    trans = natural(box_transfer)
    rtrans = natural(root_transfer)
    coup = natural(box_coupling.reshape(half_boxes * 16, 4096))
    rcoup = root_coupling[0]
    order = jnp.asarray(in_order_matrix(), BF16)
    back = jnp.asarray(in_order_matrix().T.copy(), BF16)
    spread_m = jnp.asarray(spread_matrix(), BF16)
    unfold = jnp.asarray(unfold_matrix(), BF16)

    zw, pay_low, pay_high, boxes = pl.pallas_call(
        up_kernel,
        name="up",
        out_shape=(
            shape_of((2 * tiles, 16, 128), BF16),
            shape_of((64, 16, 128), BF16),
            shape_of((64, 16, 128), BF16),
            shape_of((box_count, 16, 128), BF16),
        ),
        in_specs=[smem()] + [hbm()] * 7,
        out_specs=tuple([hbm()] * 4),
        scratch_shapes=[
            VMEM(density.shape, BF16),
            VMEM((1, points), F32),
            VMEM(coords.shape, F32),
            VMEM(basis.shape, BF16),
            VMEM(trans.shape, BF16),
            VMEM(order.shape, BF16),
            VMEM(spread_m.shape, BF16),
            VMEM((box_count * 16, 512), BF16),
            VMEM((box_count * 16, 512), BF16),
            VMEM((2 * tiles, 8, 128), F32),
            VMEM((2 * tiles, 16, 128), BF16),
            VMEM((64, 16, 128), BF16),
            VMEM((64, 16, 128), BF16),
            VMEM((box_count, 16, 128), BF16),
            pltpu.SemaphoreType.DMA((7,)),
            pltpu.SemaphoreType.DMA((4,)),
        ],
        compiler_params=params(),
    )(
        ghost_send,
        density,
        qweight.reshape(1, points),
        coords,
        basis,
        trans,
        order,
        spread_m,
    )
    root = pl.pallas_call(
        top_kernel,
        name="top",
        out_shape=shape_of((peers, 8, 128), BF16),
        in_specs=[hbm()] * 3,
        out_specs=hbm(),
        scratch_shapes=[
            VMEM(boxes.shape, BF16),
            VMEM(rtrans.shape, BF16),
            VMEM(spread_m.shape, BF16),
            VMEM((peers, 8, 128), BF16),
            pltpu.SemaphoreType.DMA((4,)),
        ],
        compiler_params=params(),
        cost_estimate=pl.CostEstimate(flops=2 * 10**10, bytes_accessed=10**6, transcendentals=0),
    )(boxes, rtrans, spread_m)
    pay_below = shifted(pay_low, 1)
    pay_above = shifted(pay_high, -1)
    roots = lax.all_to_all(root, "leaf", 0, 0, tiled=True)

    table = 2 * (tiles + 64)
    near, fields = pl.pallas_call(
        near_kernel,
        name="near",
        out_shape=(
            shape_of((half_leaves // 2, 16, 128), F32),
            shape_of((half_boxes, 32, 256), F32),
        ),
        in_specs=[smem()] * 3 + [hbm()] * 6,
        out_specs=(hbm(), hbm()),
        scratch_shapes=[
            VMEM(coords.shape, F32),
            VMEM(pay_below.shape, BF16),
            VMEM(pay_above.shape, BF16),
            VMEM(coup.shape, BF16),
            VMEM((half_leaves // 2, 16, 128), F32),
            VMEM((half_boxes, 32, 256), F32),
            VMEM((table, 48, 128), BF16),
            VMEM((table, 16, 128), BF16),
            VMEM((half_leaves * 64, 48), BF16),
            VMEM((half_leaves + 1, 16, 64), F32),
            VMEM((3 * box_count, 16, 128), BF16),
            VMEM((2, ITEMS, 64, 256), BF16),
            VMEM((2, ITEMS, 16, 256), BF16),
            VMEM((52, 16, 128), BF16),
            pltpu.SMEM((half_leaves * 3 + 3 * ITEMS + 8,), jnp.int32),
            pltpu.SemaphoreType.DMA((6,)),
            pltpu.SemaphoreType.DMA((2,)),
        ],
        compiler_params=params(),
        cost_estimate=pl.CostEstimate(
            flops=4 * 10**10, bytes_accessed=10**7, transcendentals=6 * 10**6
        ),
    )(
        near_list.T,
        near_count,
        box_list,
        zw,
        coords,
        pay_below,
        pay_above,
        boxes,
        coup,
    )

    return pl.pallas_call(
        down_kernel,
        name="down",
        out_shape=shape_of((16, half_leaves * 64), BF16),
        in_specs=[smem()] + [hbm()] * 9,
        out_specs=hbm(),
        scratch_shapes=[
            VMEM(roots.shape, BF16),
            VMEM(rcoup.shape, BF16),
            VMEM((half_boxes * 32, 128), BF16),
            VMEM(fields.shape, F32),
            VMEM((half_leaves * 32, 128), BF16),
            VMEM((half_leaves * 32, 128), BF16),
            VMEM(near.shape, F32),
            VMEM(unfold.shape, BF16),
            VMEM(back.shape, BF16),
            VMEM((16, half_leaves * 64), BF16),
            VMEM((half_boxes * 16, 128), BF16),
            VMEM((half_boxes * 16, 512), BF16),
            VMEM((half_boxes * 16, 512), BF16),
            pltpu.SemaphoreType.DMA((9,)),
            pltpu.SemaphoreType.DMA,
        ],
        compiler_params=params(),
    )(root_list, roots, rcoup, rtrans, fields, trans, basis, near, unfold, back)


def solution(mesh):
    in_specs = (
        P(None, "leaf"),
        P(None, "leaf"),
        P("leaf"),
        P("leaf", None),
        P("leaf", None),
        P("leaf", None),
        P(("leaf", "sub"), None, None),
        P("leaf", None, None),
        P(("leaf", "sub"), None),
        P(("leaf", "sub")),
        P(("leaf", "sub"), None),
        P("leaf", None),
        P("leaf", "sub", None, None),
    )
    out_specs = P(None, ("leaf", "sub"))
    return jax.shard_map(
        per_device, mesh=mesh, in_specs=in_specs, out_specs=out_specs, check_vma=False
    )
```

```python
import functools

import jax
import jax.numpy as jnp
import numpy as np
from jax import lax
from jax.experimental import pallas as pl
from jax.experimental.pallas import tpu as pltpu
from jax.sharding import PartitionSpec as P

LEAF = 64
RANK = 64
DELTA_SQ = 0.0025
UP = 16
UP_PARTS = 4
ITEMS = 16
DOWN = 8
F32 = jnp.float32
BF16 = jnp.bfloat16
VMEM = pltpu.VMEM
NT = (((1,), (1,)), ((), ()))


def in_order_matrix():
    out = np.zeros((512, 512), np.float32)
    for leaf in range(8):
        for m in range(32):
            for par in range(2):
                out[leaf * 64 + 2 * m + par, par * 256 + m * 8 + leaf] = 1
    return out


def unfold_matrix():
    out = np.zeros((512, 128), np.float32)
    for par in range(2):
        for m in range(32):
            for leaf in range(8):
                out[par * 256 + m * 8 + leaf, 2 * m + par] = 1
                out[par * 256 + m * 8 + leaf, 64 + 2 * m + par] = 1
    return out


def spread_matrix():
    out = unfold_matrix().T.copy()
    out[64:] = 0
    return out


def dot(a, b):
    return jnp.dot(a, b, preferred_element_type=F32)


def dot_t(a, b):
    return lax.dot_general(a, b, NT, preferred_element_type=F32)


def low_half(shape):
    return lax.broadcasted_iota(jnp.int32, shape, len(shape) - 1) < 64


def lane_slot(shape):
    return lax.broadcasted_iota(jnp.int32, shape, len(shape) - 1) & 7


def roll_half(value):
    return pltpu.roll(value, 64, value.ndim - 1)


def half_masks():
    low = low_half((16, 128))
    return (
        jnp.where(low, 1.0, 0.0).astype(BF16),
        jnp.where(low, 0.0, 1.0).astype(BF16),
    )


def slot_masks(rows):
    slot = lane_slot((rows, 256))
    return [jnp.where(slot == s, 1.0, 0.0).astype(BF16) for s in range(8)]


def pick_slots(parts):
    slot = lane_slot(parts[0].shape)
    out = parts[0]
    for s in range(1, 8):
        out = jnp.where(slot == s, parts[s], out)
    return out


def add_halves(value):
    chosen = jnp.where(low_half((16, 128)), value[:16], value[16:])
    return chosen + roll_half(chosen)


def gathered(wide):
    picked = pick_slots([wide[s * 16 : s * 16 + 16] for s in range(8)]).astype(BF16)
    return jnp.concatenate([picked[:, :256], picked[:, 256:]], axis=0)


def copied(pairs, sems):
    copies = [pltpu.make_async_copy(a, b, sems.at[i]) for i, (a, b) in enumerate(pairs)]
    for copy in copies:
        copy.start()
    return copies


def up_kernel(
    send,
    dens_in,
    qw_in,
    coords_in,
    basis_in,
    trans_in,
    rtrans_in,
    order_in,
    spread_in,
    zw_out,
    pay_low_out,
    pay_high_out,
    boxes_out,
    root_out,
    dens,
    qw,
    coords,
    basis,
    trans,
    rtrans,
    order,
    spread_ref,
    flat,
    ordered,
    cz,
    rolled,
    pay_low,
    pay_high,
    boxes,
    root,
    sems,
    out_sems,
):
    part = basis.shape[0] // UP_PARTS
    pairs = [
        (dens_in, dens),
        (qw_in, qw),
        (coords_in, coords),
        (order_in, order),
        (spread_in, spread_ref),
    ]
    for i in range(UP_PARTS):
        cut = pl.ds(i * part, part)
        pairs += [(basis_in.at[cut], basis.at[cut]), (trans_in.at[cut], trans.at[cut])]
    pairs.append((rtrans_in, rtrans))
    copies = copied(pairs, sems)
    for copy in copies[:3]:
        copy.wait()
    tiles = dens.shape[1] // 128
    box_count = tiles // 4
    mlo, mhi = half_masks()

    def weigh(b, carry):
        at = pl.multiple_of(b * 512, 512)
        row = pl.multiple_of(b * 16, 16)
        w = (dens[:, pl.ds(at, 512)].astype(F32) * qw[:, pl.ds(at, 512)]).astype(BF16)
        flat[pl.ds(row, 16), :] = w
        wide = w.astype(F32)
        c = coords[:, pl.ds(at, 512)]
        c = jnp.concatenate([c, jnp.zeros((5, 512), F32)], axis=0)
        for j in range(4):
            v = b * 4 + j
            cut = slice(j * 128, j * 128 + 128)
            rolled[2 * v] = w[:, cut]
            rolled[2 * v + 1] = roll_half(wide[:, cut]).astype(BF16)
            cz[2 * v] = c[:, cut]
            cz[2 * v + 1] = roll_half(c[:, cut])
        return carry

    lax.fori_loop(0, box_count, weigh, 0, unroll=8)

    kept = pltpu.make_async_copy(rolled, zw_out, out_sems.at[0])
    copies[3].wait()
    ordered[...] = dot(flat[...], order[...]).astype(BF16)

    low8 = low_half((8, 128))

    def pack(i, carry):
        for d, pay in ((0, pay_low), (1, pay_high)):
            parts = []
            for j in range(2):
                pair = i * 2 + j
                s0 = send[0, 0, d, pair * 2]
                s1 = send[0, 0, d, pair * 2 + 1]
                i0 = s0
                i1 = s1 ^ 1
                pay[pair] = rolled[i0] * mlo + rolled[i1] * mhi
                c = jnp.where(low8, cz[i0], cz[i1])
                high = c.astype(BF16).astype(F32)
                parts += [high[0:4], (c - high)[0:4]]
            pay[32 + i] = jnp.concatenate(parts, axis=0).astype(BF16)
        return carry

    lax.fori_loop(0, 16, pack, 0, unroll=8)

    masks = slot_masks(32)

    copies[4].wait()

    def up(i):
        picks = [i * UP + j for j in range(UP)]
        rows = [pl.ds(pl.multiple_of(b * 256, 256), 256) for b in picks]
        outs = []
        for b, r in zip(picks, rows):
            w = ordered[pl.ds(pl.multiple_of(b * 16, 16), 16), :]
            w = jnp.concatenate([w[:, :256], w[:, 256:]], axis=0)
            moving = jnp.concatenate([w * m for m in masks], axis=0)
            outs.append(dot(moving, basis[r, :]))
        coefs = [
            jnp.concatenate(
                [add_halves(out[s * 32 : s * 32 + 32]) for s in range(8)], axis=0
            ).astype(BF16)
            for out in outs
        ]
        wides = [dot(c, spread_ref[...]) for c in coefs]
        lifted = [dot(gathered(w), trans[r, :]) for w, r in zip(wides, rows)]
        for b, total in zip(picks, lifted):
            boxes[b] = add_halves(total).astype(BF16)

    steps = box_count // UP
    waits = 2 * UP_PARTS // steps
    for i in range(steps):
        for copy in copies[5 + i * waits : 5 + i * waits + waits]:
            copy.wait()
        up(i)
        if i == 0:
            kept.start()

    def finish(i, carry):
        pair = boxes[2 * i] * mlo + boxes[2 * i + 1] * mhi
        pay_low[48 + i] = pair
        pay_high[48 + i] = pair
        return carry

    lax.fori_loop(0, box_count // 2, finish, 0, unroll=4)

    sends = [
        pltpu.make_async_copy(a, b, out_sems.at[i])
        for i, (a, b) in ((1, (pay_low, pay_low_out)), (2, (pay_high, pay_high_out)), (3, (boxes, boxes_out)))
    ]
    for copy in sends:
        copy.start()
    copies[-1].wait()
    wides = [
        dot(jnp.concatenate([boxes[g * 8 + s] for s in range(8)], axis=0), spread_ref[...])
        for g in range(box_count // 8)
    ]
    total = jnp.zeros((32, 128), F32)
    for g, wide in enumerate(wides):
        total += dot(gathered(wide), rtrans[g * 256 : g * 256 + 256, :])
    total = add_halves(total)
    total = jnp.where(low8, total[:8], total[8:]).astype(BF16)

    def copy_root(i, carry):
        root[i] = total
        return carry

    lax.fori_loop(0, root.shape[0], copy_root, 0, unroll=16)
    last = pltpu.make_async_copy(root, root_out, out_sems.at[4])
    last.start()
    for copy in sends + [kept, last]:
        copy.wait()


def split3(value):
    high = value.astype(BF16).astype(F32)
    rest = value - high
    mid = rest.astype(BF16).astype(F32)
    return high, mid, rest - mid


def near_kernel(
    near,
    count,
    box_list,
    zw,
    coords_in,
    pay_below,
    pay_above,
    boxes,
    coup_in,
    near_hbm,
    fields_hbm,
    coords,
    extra_below,
    extra_above,
    coup,
    near_out,
    fields,
    feats,
    wz,
    tt,
    acc,
    ab,
    kernels,
    weights,
    live_masks,
    slots,
    sems,
    out_sems,
):
    half_leaves = count.shape[0]
    own_tiles = zw.shape[0] // 2
    ghost = 32
    half_tiles = own_tiles // 2
    mlo, mhi = half_masks()
    own_boxes = boxes.shape[0]
    copies = copied(
        (
            (coords_in, coords),
            (zw, wz.at[pl.ds(0, 2 * own_tiles)]),
            (pay_below, extra_below),
            (pay_above, extra_above),
            (boxes, ab.at[pl.ds(0, own_boxes)]),
            (coup_in, coup),
        ),
        sems,
    )

    def listing(t, listed):
        for k in range(3):
            slots[listed + k] = t * 516 + k
        return listed + ((count[t] + 3) >> 2)

    listed = lax.fori_loop(0, half_leaves, listing, 0, unroll=8)
    for k in range(3 * ITEMS):
        slots[listed + k] = half_leaves * 512
    rounds = (listed + 2 * ITEMS - 1) // (2 * ITEMS)

    def clear(i, carry):
        acc[i] = jnp.zeros((16, 64), F32)
        return carry

    lax.fori_loop(0, 2 * half_tiles + 1, clear, 0, unroll=8)

    for n in range(13):
        for k in range(4):
            part = (mlo, mhi)[k % 2]
            live_masks[n * 4 + k] = part if k < n else jnp.zeros_like(part)

    def source_pair(e0, e1):
        one = feats[e0]
        two = feats[e1 ^ 1]
        return jnp.concatenate(
            [one[r : r + 16] * mlo + two[r : r + 16] * mhi for r in range(0, 48, 16)], axis=0
        )

    def weight_pair(e0, e1, at):
        return wz[e0] * live_masks[at] + wz[e1 ^ 1] * live_masks[at + 1]

    def first(group, buffer):
        squares = []
        for j in range(ITEMS):
            v = slots[group * ITEMS + j]
            t = (v >> 2) & (half_leaves - 1)
            at = (v & 3) * 4
            live = (count[t] - at) * 4
            e = [near[at + k, t] for k in range(4)]
            source = jnp.concatenate([source_pair(e[0], e[1]), source_pair(e[2], e[3])], axis=1)
            weights[buffer, j] = jnp.concatenate(
                [weight_pair(e[0], e[1], live), weight_pair(e[2], e[3], live + 2)], axis=1
            )
            squares.append(dot(tt[pl.ds(pl.multiple_of(t * 64, 64), 64), :], source))
        for j, square in enumerate(squares):
            kernels[buffer, j] = lax.rsqrt(square).astype(BF16)

    def second(group, buffer):
        values = [dot_t(weights[buffer, j], kernels[buffer, j]) for j in range(ITEMS)]
        for j, value in enumerate(values):
            acc[slots[group * ITEMS + j] >> 9] += value

    copies[0].wait()
    row8 = lax.broadcasted_iota(jnp.int32, (8, 128), 0)

    def put_source(v, c):
        c = jnp.where(row8 < 3, c - 0.5, 0.0)
        size = jnp.sum(c * c, axis=0, keepdims=True)
        u = jnp.where(row8 < 3, c, jnp.where(row8 == 3, size, jnp.where(row8 == 4, 1.0, 0.0)))
        for at, block in ((2 * v, u), (2 * v + 1, roll_half(u))):
            h, m, l = split3(block)
            feats[at] = jnp.concatenate([h, m, l, h, m, h], axis=0).astype(BF16)

    def own(i, carry):
        for j in range(16):
            v = i * 16 + j
            c = coords[:, pl.ds(pl.multiple_of(v * 128, 128), 128)]
            c = jnp.concatenate([c, jnp.zeros((5, 128), F32)], axis=0)
            put_source(v, c)
        return carry

    lax.fori_loop(0, own_tiles // 16, own, 0)
    eye = jnp.where(
        lax.broadcasted_iota(jnp.int32, (128, 128), 0)
        == lax.broadcasted_iota(jnp.int32, (128, 128), 1),
        1.0,
        0.0,
    ).astype(BF16)
    first_tile = lax.axis_index("sub") * half_tiles

    def target(i, carry):
        blocks = []
        for j in range(16):
            v = i * 16 + j
            c = coords[:, pl.ds(pl.multiple_of((first_tile + v) * 128, 128), 128)]
            c = jnp.concatenate([c, jnp.zeros((5, 128), F32)], axis=0)
            c = jnp.where(row8 < 3, c - 0.5, 0.0)
            size = jnp.sum(c * c, axis=0, keepdims=True) + DELTA_SQ
            u = jnp.where(
                row8 < 3, -2.0 * c, jnp.where(row8 == 3, 1.0, jnp.where(row8 == 4, size, 0.0))
            )
            h, m, l = split3(u)
            blocks.append(jnp.concatenate([h, h, h, m, m, l], axis=0).astype(BF16))
        for j, turned in enumerate([dot_t(eye, block) for block in blocks]):
            tt[pl.ds(pl.multiple_of((i * 16 + j) * 128, 128), 128), :] = turned.astype(BF16)
        return carry

    lax.fori_loop(0, half_tiles // 16, target, 0)

    for copy in copies[1:4]:
        copy.wait()
    for base, pay in ((own_tiles, extra_below), (own_tiles + ghost, extra_above)):

        def ghosts(i, carry, base=base, pay=pay):
            both = pay[32 + i].astype(F32)
            for j in range(2):
                v = i * 2 + j
                c = both[j * 8 : j * 8 + 4] + both[j * 8 + 4 : j * 8 + 8]
                c = jnp.concatenate([c, jnp.zeros((4, 128), F32)], axis=0)
                put_source(base + v, c)
                wz[2 * (base + v)] = pay[v]
                wz[2 * (base + v) + 1] = roll_half(pay[v].astype(F32)).astype(BF16)
            return carry

        lax.fori_loop(0, ghost // 2, ghosts, 0, unroll=8)

    for copy in copies[4:]:
        copy.wait()
    low16 = low_half((16, 128))
    for base, pay in ((own_boxes, extra_below), (2 * own_boxes, extra_above)):

        def ghost_box(i, carry, base=base, pay=pay):
            pair = pay[48 + i].astype(F32)
            turned = roll_half(pair)
            ab[base + 2 * i] = jnp.where(low16, pair, turned).astype(BF16)
            ab[base + 2 * i + 1] = jnp.where(low16, turned, pair).astype(BF16)
            return carry

        lax.fori_loop(0, own_boxes // 2, ghost_box, 0, unroll=16)

    def couple(b, carry):
        total = None
        for kg in range(2):
            rows = []
            for k in range(8):
                source = ab[box_list[b, kg * 8 + k]]
                rows += [source * mlo, source * mhi]
            at = pl.ds(pl.multiple_of((b * 2 + kg) * 256, 256), 256)
            wide = dot_t(jnp.concatenate(rows, axis=0), coup[at, :])
            part = pick_slots([wide[s * 32 : s * 32 + 32] for s in range(8)])
            total = part if total is None else total + part
        fields[b] = total
        return carry

    lax.fori_loop(0, fields.shape[0], couple, 0, unroll=8)
    coupled = pltpu.make_async_copy(fields, fields_hbm, out_sems.at[1])
    coupled.start()

    first(0, 0)

    def items(i, carry):
        first(2 * i + 1, 1)
        second(2 * i, 0)
        first(2 * i + 2, 0)
        second(2 * i + 1, 1)
        return carry

    lax.fori_loop(0, rounds, items, 0)

    def join(v, carry):
        near_out[v] = jnp.concatenate([acc[2 * v], acc[2 * v + 1]], axis=1)
        return carry

    lax.fori_loop(0, half_tiles, join, 0, unroll=16)

    last = pltpu.make_async_copy(near_out, near_hbm, out_sems.at[0])
    last.start()
    coupled.wait()
    last.wait()


def fold(parts, unfold):
    rows = [jnp.concatenate([p[:16], p[16:]], axis=1) for p in parts]
    high = [r.astype(BF16) for r in rows]
    low = [(r - h.astype(F32)).astype(BF16) for r, h in zip(rows, high)]
    out = dot(jnp.concatenate(high + low, axis=0), unfold[...])
    n = 16 * len(parts)
    return out[:n] + out[n:]


def down_kernel(
    root_list,
    roots_in,
    rcoup_in,
    rtrans_in,
    fields_in,
    trans_in,
    basis_in,
    near_in,
    unfold_in,
    back_in,
    out_hbm,
    roots,
    rcoup,
    rtrans,
    fields,
    trans,
    basis,
    near,
    unfold,
    back,
    out,
    bf,
    far_high,
    far_low,
    sems,
    out_sems,
):
    def half_of(ref, rows):
        return ref.at[pl.ds(pl.multiple_of(lax.axis_index("sub") * rows, rows), rows)]

    pairs = [
        (roots_in, roots),
        (rcoup_in, rcoup),
        (unfold_in, unfold),
        (half_of(rtrans_in, rtrans.shape[0]), rtrans),
        (fields_in, fields),
    ]
    part = DOWN * 256
    parts = trans.shape[0] // part
    trans_half = half_of(trans_in, trans.shape[0])
    basis_half = half_of(basis_in, basis.shape[0])
    for i in range(parts):
        cut = pl.ds(i * part, part)
        pairs += [(trans_half.at[cut], trans.at[cut]), (basis_half.at[cut], basis.at[cut])]
    pairs += [(back_in, back), (near_in, near)]
    copies = copied(pairs, sems)
    for copy in copies[:3]:
        copy.wait()
    mlo, mhi = half_masks()
    low8 = low_half((8, 128))
    half_boxes = fields.shape[0]

    total = None
    known = rcoup.shape[0]
    for kg in range(2):
        rows = []
        have = min(known - kg * 8, 8)
        blocks = []
        for m in range(32):
            block = rcoup[:, m * 128 : m * 128 + 128].astype(F32)[kg * 8 : kg * 8 + have]
            if have < 8:
                block = jnp.concatenate([block, jnp.zeros((8 - have, 128), F32)], axis=0)
            blocks.append(block)
        matrix = jnp.concatenate(blocks, axis=0).astype(BF16)
        for k in range(8):
            if kg * 8 + k < known:
                source = roots[root_list[0, kg * 8 + k]].astype(F32)
                turned = roll_half(source)
                even = jnp.concatenate([source, turned], axis=0).astype(BF16) * mlo
                odd = jnp.concatenate([turned, source], axis=0).astype(BF16) * mhi
                rows += [even, odd]
            else:
                rows.append(jnp.zeros((32, 128), BF16))
        wide = dot_t(jnp.concatenate(rows, axis=0), matrix)
        part = pick_slots([wide[s * 32 : s * 32 + 32] for s in range(8)])
        total = part if total is None else total + part
    rf = fold([total], unfold).astype(BF16)
    moving = jnp.concatenate([rf * mlo, rf * mhi], axis=0)
    slot = lane_slot((32, 256))
    for copy in copies[3:5]:
        copy.wait()
    for g in range(half_boxes // 8):
        pushed = dot_t(moving, rtrans[g * 256 : g * 256 + 256, :])
        sums = [fields[g * 8 + s] + jnp.where(slot == s, pushed, 0.0) for s in range(8)]
        bf[g * 128 : g * 128 + 128, :] = fold(sums, unfold).astype(BF16)

    masks = slot_masks(16)

    def leaves(i):
        picks = [i * DOWN + j for j in range(DOWN)]
        rows = [pl.ds(pl.multiple_of(b * 256, 256), 256) for b in picks]
        spots = [pl.ds(pl.multiple_of(b * 16, 16), 16) for b in picks]
        hs = []
        for r, at in zip(rows, spots):
            field = bf[at, :]
            moving = jnp.concatenate([field * mlo, field * mhi], axis=0)
            hs.append(dot_t(moving, trans[r, :]).astype(BF16))
        wides = [
            jnp.concatenate(
                [jnp.concatenate([h[:16] * m, h[16:] * m], axis=1) for m in masks], axis=0
            )
            for h in hs
        ]
        lfs = [dot(wide, unfold[...]).astype(BF16) for wide in wides]
        fars = []
        for lf, r in zip(lfs, rows):
            parts = []
            for s in range(8):
                one = lf[s * 16 : s * 16 + 16]
                parts += [one * mlo, one * mhi]
            fars.append(dot_t(jnp.concatenate(parts, axis=0), basis[r, :]))
        for far, at in zip(fars, spots):
            far = pick_slots([far[s * 32 : s * 32 + 32] for s in range(8)])
            far = jnp.concatenate([far[:16], far[16:]], axis=1)
            high = far.astype(BF16)
            far_high[at, :] = high
            far_low[at, :] = (far - high.astype(F32)).astype(BF16)

    for i in range(parts):
        for copy in copies[5 + 2 * i : 7 + 2 * i]:
            copy.wait()
        leaves(i)

    for copy in copies[-2:]:
        copy.wait()

    def emit(i):
        at = pl.ds(i * 64, 64)
        far = dot(far_high[at, :], back[...]) + dot(far_low[at, :], back[...])
        for b in range(4):
            for j in range(4):
                v = (i * 4 + b) * 4 + j
                value = far[b * 16 : b * 16 + 16, j * 128 : j * 128 + 128] + near[v]
                out[:, pl.ds(v * 128, 128)] = value.astype(BF16)

    sends = []
    for i in range(half_boxes // 4):
        emit(i)
        cut = pl.ds(i * 2048, 2048)
        sends.append(pltpu.make_async_copy(out.at[:, cut], out_hbm.at[:, cut], out_sems.at[i]))
        sends[i].start()
    for send in sends:
        send.wait()


def natural(matrices):
    n = matrices.shape[0]
    return jnp.transpose(matrices.reshape(n // 8, 8, 32, 128), (0, 2, 1, 3)).reshape(n * 32, 128)


def whole(shape=None):
    return pl.BlockSpec(memory_space=VMEM)


def smem():
    return pl.BlockSpec(memory_space=pltpu.SMEM)


def shape_of(shape, dtype):
    return jax.ShapeDtypeStruct(shape, dtype)


def hbm():
    return pl.BlockSpec(memory_space=pltpu.HBM)


def params():
    return pltpu.CompilerParams(vmem_limit_bytes=66_900_000)


def shifted(value, by):
    peers = lax.axis_size("leaf")
    pairs = [(i, i + by) for i in range(peers) if 0 <= i + by < peers]
    return lax.ppermute(value, "leaf", pairs)


def per_device(
    density,
    coords,
    qweight,
    leaf_basis,
    box_transfer,
    root_transfer,
    box_coupling,
    root_coupling,
    near_list,
    near_count,
    box_list,
    root_list,
    ghost_send,
):
    points = density.shape[1]
    peers = lax.axis_size("leaf")
    tiles = points // 128
    box_count = tiles // 4
    half_leaves = near_list.shape[0]
    half_boxes = box_list.shape[0]
    basis = natural(leaf_basis)
    trans = natural(box_transfer)
    rtrans = natural(root_transfer)
    coup = natural(box_coupling.reshape(half_boxes * 16, 4096))
    rcoup = root_coupling[0]
    order = jnp.asarray(in_order_matrix(), BF16)
    back = jnp.asarray(in_order_matrix().T.copy(), BF16)
    spread_m = jnp.asarray(spread_matrix(), BF16)
    unfold = jnp.asarray(unfold_matrix(), BF16)

    zw, pay_low, pay_high, boxes, root = pl.pallas_call(
        up_kernel,
        name="up",
        out_shape=(
            shape_of((2 * tiles, 16, 128), BF16),
            shape_of((64, 16, 128), BF16),
            shape_of((64, 16, 128), BF16),
            shape_of((box_count, 16, 128), BF16),
            shape_of((peers, 8, 128), BF16),
        ),
        in_specs=[smem()] + [hbm()] * 8,
        out_specs=tuple([hbm()] * 5),
        scratch_shapes=[
            VMEM(density.shape, BF16),
            VMEM((1, points), F32),
            VMEM(coords.shape, F32),
            VMEM(basis.shape, BF16),
            VMEM(trans.shape, BF16),
            VMEM(rtrans.shape, BF16),
            VMEM(order.shape, BF16),
            VMEM(spread_m.shape, BF16),
            VMEM((box_count * 16, 512), BF16),
            VMEM((box_count * 16, 512), BF16),
            VMEM((2 * tiles, 8, 128), F32),
            VMEM((2 * tiles, 16, 128), BF16),
            VMEM((64, 16, 128), BF16),
            VMEM((64, 16, 128), BF16),
            VMEM((box_count, 16, 128), BF16),
            VMEM((peers, 8, 128), BF16),
            pltpu.SemaphoreType.DMA((6 + 2 * UP_PARTS,)),
            pltpu.SemaphoreType.DMA((5,)),
        ],
        compiler_params=params(),
    )(
        ghost_send,
        density,
        qweight.reshape(1, points),
        coords,
        basis,
        trans,
        rtrans,
        order,
        spread_m,
    )
    pay_below = shifted(pay_low, 1)
    pay_above = shifted(pay_high, -1)
    roots = lax.all_to_all(root, "leaf", 0, 0, tiled=True)

    table = 2 * (tiles + 64)
    near, fields = pl.pallas_call(
        near_kernel,
        name="near",
        out_shape=(
            shape_of((half_leaves // 2, 16, 128), F32),
            shape_of((half_boxes, 32, 256), F32),
        ),
        in_specs=[smem()] * 3 + [hbm()] * 6,
        out_specs=(hbm(), hbm()),
        scratch_shapes=[
            VMEM(coords.shape, F32),
            VMEM(pay_below.shape, BF16),
            VMEM(pay_above.shape, BF16),
            VMEM(coup.shape, BF16),
            VMEM((half_leaves // 2, 16, 128), F32),
            VMEM((half_boxes, 32, 256), F32),
            VMEM((table, 48, 128), BF16),
            VMEM((table, 16, 128), BF16),
            VMEM((half_leaves * 64, 48), BF16),
            VMEM((half_leaves + 1, 16, 64), F32),
            VMEM((3 * box_count, 16, 128), BF16),
            VMEM((2, ITEMS, 64, 256), BF16),
            VMEM((2, ITEMS, 16, 256), BF16),
            VMEM((52, 16, 128), BF16),
            pltpu.SMEM((half_leaves * 3 + 3 * ITEMS + 8,), jnp.int32),
            pltpu.SemaphoreType.DMA((6,)),
            pltpu.SemaphoreType.DMA((2,)),
        ],
        compiler_params=params(),
        cost_estimate=pl.CostEstimate(
            flops=4 * 10**10, bytes_accessed=10**7, transcendentals=6 * 10**6
        ),
    )(
        near_list.T,
        near_count,
        box_list,
        zw,
        coords,
        pay_below,
        pay_above,
        boxes,
        coup,
    )

    return pl.pallas_call(
        down_kernel,
        name="down",
        out_shape=shape_of((16, half_leaves * 64), BF16),
        in_specs=[smem()] + [hbm()] * 9,
        out_specs=hbm(),
        scratch_shapes=[
            VMEM(roots.shape, BF16),
            VMEM(rcoup.shape, BF16),
            VMEM((half_boxes * 32, 128), BF16),
            VMEM(fields.shape, F32),
            VMEM((half_leaves * 32, 128), BF16),
            VMEM((half_leaves * 32, 128), BF16),
            VMEM(near.shape, F32),
            VMEM(unfold.shape, BF16),
            VMEM(back.shape, BF16),
            VMEM((16, half_leaves * 64), BF16),
            VMEM((half_boxes * 16, 128), BF16),
            VMEM((half_boxes * 16, 512), BF16),
            VMEM((half_boxes * 16, 512), BF16),
            pltpu.SemaphoreType.DMA((7 + 2 * (half_boxes // DOWN),)),
            pltpu.SemaphoreType.DMA((half_boxes // 4,)),
        ],
        compiler_params=params(),
    )(root_list, roots, rcoup, rtrans, fields, trans, basis, near, unfold, back)


def solution(mesh):
    in_specs = (
        P(None, "leaf"),
        P(None, "leaf"),
        P("leaf"),
        P("leaf", None),
        P("leaf", None),
        P("leaf", None),
        P(("leaf", "sub"), None, None),
        P("leaf", None, None),
        P(("leaf", "sub"), None),
        P(("leaf", "sub")),
        P(("leaf", "sub"), None),
        P("leaf", None),
        P("leaf", "sub", None, None),
    )
    out_specs = P(None, ("leaf", "sub"))
    return jax.shard_map(
        per_device, mesh=mesh, in_specs=in_specs, out_specs=out_specs, check_vma=False
    )
```

```python
import functools

import jax
import jax.numpy as jnp
import numpy as np
from jax import lax
from jax.experimental import pallas as pl
from jax.experimental.pallas import tpu as pltpu
from jax.sharding import PartitionSpec as P

LEAF = 64
RANK = 64
DELTA_SQ = 0.0025
UP = 16
UP_PARTS = 4
ITEMS = 16
DOWN = 8
F32 = jnp.float32
BF16 = jnp.bfloat16
VMEM = pltpu.VMEM
NT = (((1,), (1,)), ((), ()))


def in_order_matrix():
    out = np.zeros((512, 512), np.float32)
    for leaf in range(8):
        for m in range(32):
            for par in range(2):
                out[leaf * 64 + 2 * m + par, par * 256 + m * 8 + leaf] = 1
    return out


def unfold_matrix():
    out = np.zeros((512, 128), np.float32)
    for par in range(2):
        for m in range(32):
            for leaf in range(8):
                out[par * 256 + m * 8 + leaf, 2 * m + par] = 1
                out[par * 256 + m * 8 + leaf, 64 + 2 * m + par] = 1
    return out


def spread_matrix():
    out = unfold_matrix().T.copy()
    out[64:] = 0
    return out


def dot(a, b):
    return jnp.dot(a, b, preferred_element_type=F32)


def dot_t(a, b):
    return lax.dot_general(a, b, NT, preferred_element_type=F32)


def low_half(shape):
    return lax.broadcasted_iota(jnp.int32, shape, len(shape) - 1) < 64


def lane_slot(shape):
    return lax.broadcasted_iota(jnp.int32, shape, len(shape) - 1) & 7


def roll_half(value):
    return pltpu.roll(value, 64, value.ndim - 1)


def half_masks():
    low = low_half((16, 128))
    return (
        jnp.where(low, 1.0, 0.0).astype(BF16),
        jnp.where(low, 0.0, 1.0).astype(BF16),
    )


def slot_masks(rows):
    slot = lane_slot((rows, 256))
    return [jnp.where(slot == s, 1.0, 0.0).astype(BF16) for s in range(8)]


def pick_slots(parts):
    slot = lane_slot(parts[0].shape)
    out = parts[0]
    for s in range(1, 8):
        out = jnp.where(slot == s, parts[s], out)
    return out


def add_halves(value):
    chosen = jnp.where(low_half((16, 128)), value[:16], value[16:])
    return chosen + roll_half(chosen)


def gathered(wide):
    picked = pick_slots([wide[s * 16 : s * 16 + 16] for s in range(8)]).astype(BF16)
    return jnp.concatenate([picked[:, :256], picked[:, 256:]], axis=0)


def copied(pairs, sems):
    copies = [pltpu.make_async_copy(a, b, sems.at[i]) for i, (a, b) in enumerate(pairs)]
    for copy in copies:
        copy.start()
    return copies


def up_kernel(
    send,
    dens_in,
    qw_in,
    coords_in,
    basis_in,
    trans_in,
    rtrans_in,
    order_in,
    spread_in,
    zw_out,
    pay_one_out,
    pay_two_out,
    boxes_out,
    root_out,
    dens,
    qw,
    coords,
    basis,
    trans,
    rtrans,
    order,
    spread_ref,
    flat,
    ordered,
    cz,
    rolled,
    pay_one,
    pay_two,
    boxes,
    root,
    sems,
    out_sems,
):
    part = basis.shape[0] // UP_PARTS
    pairs = [
        (dens_in, dens),
        (qw_in, qw),
        (coords_in, coords),
        (order_in, order),
        (spread_in, spread_ref),
    ]
    for i in range(UP_PARTS):
        cut = pl.ds(i * part, part)
        pairs += [(basis_in.at[cut], basis.at[cut]), (trans_in.at[cut], trans.at[cut])]
    pairs.append((rtrans_in, rtrans))
    copies = copied(pairs, sems)
    for copy in copies[:3]:
        copy.wait()
    tiles = dens.shape[1] // 128
    box_count = tiles // 4
    mlo, mhi = half_masks()

    def weigh(b, carry):
        at = pl.multiple_of(b * 512, 512)
        row = pl.multiple_of(b * 16, 16)
        w = (dens[:, pl.ds(at, 512)].astype(F32) * qw[:, pl.ds(at, 512)]).astype(BF16)
        flat[pl.ds(row, 16), :] = w
        wide = w.astype(F32)
        c = coords[:, pl.ds(at, 512)]
        c = jnp.concatenate([c, jnp.zeros((5, 512), F32)], axis=0)
        for j in range(4):
            v = b * 4 + j
            cut = slice(j * 128, j * 128 + 128)
            rolled[2 * v] = w[:, cut]
            rolled[2 * v + 1] = roll_half(wide[:, cut]).astype(BF16)
            cz[2 * v] = c[:, cut]
            cz[2 * v + 1] = roll_half(c[:, cut])
        return carry

    lax.fori_loop(0, box_count, weigh, 0, unroll=8)

    kept = pltpu.make_async_copy(rolled, zw_out, out_sems.at[0])
    copies[3].wait()
    ordered[...] = dot(flat[...], order[...]).astype(BF16)

    low8 = low_half((8, 128))
    odd = lax.axis_index("leaf") & 1

    def pack(i, carry):
        for d, pay in ((odd, pay_one), (1 - odd, pay_two)):
            parts = []
            for j in range(2):
                pair = i * 2 + j
                s0 = send[0, 0, d, pair * 2]
                s1 = send[0, 0, d, pair * 2 + 1]
                i0 = s0
                i1 = s1 ^ 1
                pay[pair] = rolled[i0] * mlo + rolled[i1] * mhi
                c = jnp.where(low8, cz[i0], cz[i1])
                high = c.astype(BF16).astype(F32)
                parts += [high[0:4], (c - high)[0:4]]
            pay[32 + i] = jnp.concatenate(parts, axis=0).astype(BF16)
        return carry

    lax.fori_loop(0, 16, pack, 0, unroll=8)

    masks = slot_masks(32)

    copies[4].wait()

    def up(i):
        picks = [i * UP + j for j in range(UP)]
        rows = [pl.ds(pl.multiple_of(b * 256, 256), 256) for b in picks]
        outs = []
        for b, r in zip(picks, rows):
            w = ordered[pl.ds(pl.multiple_of(b * 16, 16), 16), :]
            w = jnp.concatenate([w[:, :256], w[:, 256:]], axis=0)
            moving = jnp.concatenate([w * m for m in masks], axis=0)
            outs.append(dot(moving, basis[r, :]))
        coefs = [
            jnp.concatenate(
                [add_halves(out[s * 32 : s * 32 + 32]) for s in range(8)], axis=0
            ).astype(BF16)
            for out in outs
        ]
        wides = [dot(c, spread_ref[...]) for c in coefs]
        lifted = [dot(gathered(w), trans[r, :]) for w, r in zip(wides, rows)]
        for b, total in zip(picks, lifted):
            boxes[b] = add_halves(total).astype(BF16)

    steps = box_count // UP
    waits = 2 * UP_PARTS // steps
    for i in range(steps):
        for copy in copies[5 + i * waits : 5 + i * waits + waits]:
            copy.wait()
        up(i)
        if i == 0:
            kept.start()

    def finish(i, carry):
        pair = boxes[2 * i] * mlo + boxes[2 * i + 1] * mhi
        pay_one[48 + i] = pair
        pay_two[48 + i] = pair
        return carry

    lax.fori_loop(0, box_count // 2, finish, 0, unroll=4)

    sends = [
        pltpu.make_async_copy(a, b, out_sems.at[i])
        for i, (a, b) in ((1, (pay_one, pay_one_out)), (2, (pay_two, pay_two_out)), (3, (boxes, boxes_out)))
    ]
    for copy in sends:
        copy.start()
    copies[-1].wait()
    wides = [
        dot(jnp.concatenate([boxes[g * 8 + s] for s in range(8)], axis=0), spread_ref[...])
        for g in range(box_count // 8)
    ]
    total = jnp.zeros((32, 128), F32)
    for g, wide in enumerate(wides):
        total += dot(gathered(wide), rtrans[g * 256 : g * 256 + 256, :])
    total = add_halves(total)
    total = jnp.where(low8, total[:8], total[8:]).astype(BF16)

    def copy_root(i, carry):
        root[i] = total
        return carry

    lax.fori_loop(0, root.shape[0], copy_root, 0, unroll=16)
    last = pltpu.make_async_copy(root, root_out, out_sems.at[4])
    last.start()
    for copy in sends + [kept, last]:
        copy.wait()


def split3(value):
    high = value.astype(BF16).astype(F32)
    rest = value - high
    mid = rest.astype(BF16).astype(F32)
    return high, mid, rest - mid


def near_kernel(
    near,
    count,
    box_list,
    zw,
    coords_in,
    got_one,
    got_two,
    boxes,
    coup_in,
    near_hbm,
    fields_hbm,
    coords,
    extra_one,
    extra_two,
    coup,
    near_out,
    fields,
    feats,
    wz,
    tt,
    acc,
    ab,
    kernels,
    weights,
    live_masks,
    slots,
    sems,
    out_sems,
):
    half_leaves = count.shape[0]
    own_tiles = zw.shape[0] // 2
    ghost = 32
    half_tiles = own_tiles // 2
    mlo, mhi = half_masks()
    own_boxes = boxes.shape[0]
    copies = copied(
        (
            (coords_in, coords),
            (zw, wz.at[pl.ds(0, 2 * own_tiles)]),
            (got_one, extra_one),
            (got_two, extra_two),
            (boxes, ab.at[pl.ds(0, own_boxes)]),
            (coup_in, coup),
        ),
        sems,
    )

    def listing(t, listed):
        for k in range(3):
            slots[listed + k] = t * 516 + k
        return listed + ((count[t] + 3) >> 2)

    listed = lax.fori_loop(0, half_leaves, listing, 0, unroll=8)
    for k in range(3 * ITEMS):
        slots[listed + k] = half_leaves * 512
    rounds = (listed + 2 * ITEMS - 1) // (2 * ITEMS)

    def clear(i, carry):
        acc[i] = jnp.zeros((16, 64), F32)
        return carry

    lax.fori_loop(0, 2 * half_tiles + 1, clear, 0, unroll=8)

    for n in range(13):
        for k in range(4):
            part = (mlo, mhi)[k % 2]
            live_masks[n * 4 + k] = part if k < n else jnp.zeros_like(part)

    def source_pair(e0, e1):
        one = feats[e0]
        two = feats[e1 ^ 1]
        return jnp.concatenate(
            [one[r : r + 16] * mlo + two[r : r + 16] * mhi for r in range(0, 48, 16)], axis=0
        )

    def weight_pair(e0, e1, at):
        return wz[e0] * live_masks[at] + wz[e1 ^ 1] * live_masks[at + 1]

    def first(group, buffer):
        squares = []
        for j in range(ITEMS):
            v = slots[group * ITEMS + j]
            t = (v >> 2) & (half_leaves - 1)
            at = (v & 3) * 4
            live = (count[t] - at) * 4
            e = [near[at + k, t] for k in range(4)]
            source = jnp.concatenate([source_pair(e[0], e[1]), source_pair(e[2], e[3])], axis=1)
            weights[buffer, j] = jnp.concatenate(
                [weight_pair(e[0], e[1], live), weight_pair(e[2], e[3], live + 2)], axis=1
            )
            squares.append(dot(tt[pl.ds(pl.multiple_of(t * 64, 64), 64), :], source))
        for j, square in enumerate(squares):
            kernels[buffer, j] = lax.rsqrt(square).astype(BF16)

    def second(group, buffer):
        values = [dot_t(weights[buffer, j], kernels[buffer, j]) for j in range(ITEMS)]
        for j, value in enumerate(values):
            acc[slots[group * ITEMS + j] >> 9] += value

    copies[0].wait()
    row8 = lax.broadcasted_iota(jnp.int32, (8, 128), 0)

    def put_source(v, c):
        c = jnp.where(row8 < 3, c - 0.5, 0.0)
        size = jnp.sum(c * c, axis=0, keepdims=True)
        u = jnp.where(row8 < 3, c, jnp.where(row8 == 3, size, jnp.where(row8 == 4, 1.0, 0.0)))
        for at, block in ((2 * v, u), (2 * v + 1, roll_half(u))):
            h, m, l = split3(block)
            feats[at] = jnp.concatenate([h, m, l, h, m, h], axis=0).astype(BF16)

    def own(i, carry):
        for j in range(16):
            v = i * 16 + j
            c = coords[:, pl.ds(pl.multiple_of(v * 128, 128), 128)]
            c = jnp.concatenate([c, jnp.zeros((5, 128), F32)], axis=0)
            put_source(v, c)
        return carry

    lax.fori_loop(0, own_tiles // 16, own, 0)
    eye = jnp.where(
        lax.broadcasted_iota(jnp.int32, (128, 128), 0)
        == lax.broadcasted_iota(jnp.int32, (128, 128), 1),
        1.0,
        0.0,
    ).astype(BF16)
    first_tile = lax.axis_index("sub") * half_tiles

    def target(i, carry):
        blocks = []
        for j in range(16):
            v = i * 16 + j
            c = coords[:, pl.ds(pl.multiple_of((first_tile + v) * 128, 128), 128)]
            c = jnp.concatenate([c, jnp.zeros((5, 128), F32)], axis=0)
            c = jnp.where(row8 < 3, c - 0.5, 0.0)
            size = jnp.sum(c * c, axis=0, keepdims=True) + DELTA_SQ
            u = jnp.where(
                row8 < 3, -2.0 * c, jnp.where(row8 == 3, 1.0, jnp.where(row8 == 4, size, 0.0))
            )
            h, m, l = split3(u)
            blocks.append(jnp.concatenate([h, h, h, m, m, l], axis=0).astype(BF16))
        for j, turned in enumerate([dot_t(eye, block) for block in blocks]):
            tt[pl.ds(pl.multiple_of((i * 16 + j) * 128, 128), 128), :] = turned.astype(BF16)
        return carry

    lax.fori_loop(0, half_tiles // 16, target, 0)

    for copy in copies[1:4]:
        copy.wait()
    odd = lax.axis_index("leaf") & 1
    for base, pay in (
        (own_tiles + ghost * (1 - odd), extra_one),
        (own_tiles + ghost * odd, extra_two),
    ):

        def ghosts(i, carry, base=base, pay=pay):
            both = pay[32 + i].astype(F32)
            for j in range(2):
                v = i * 2 + j
                c = both[j * 8 : j * 8 + 4] + both[j * 8 + 4 : j * 8 + 8]
                c = jnp.concatenate([c, jnp.zeros((4, 128), F32)], axis=0)
                put_source(base + v, c)
                wz[2 * (base + v)] = pay[v]
                wz[2 * (base + v) + 1] = roll_half(pay[v].astype(F32)).astype(BF16)
            return carry

        lax.fori_loop(0, ghost // 2, ghosts, 0, unroll=8)

    for copy in copies[4:]:
        copy.wait()
    low16 = low_half((16, 128))
    for base, pay in (
        (own_boxes * (2 - odd), extra_one),
        (own_boxes * (1 + odd), extra_two),
    ):

        def ghost_box(i, carry, base=base, pay=pay):
            pair = pay[48 + i].astype(F32)
            turned = roll_half(pair)
            ab[base + 2 * i] = jnp.where(low16, pair, turned).astype(BF16)
            ab[base + 2 * i + 1] = jnp.where(low16, turned, pair).astype(BF16)
            return carry

        lax.fori_loop(0, own_boxes // 2, ghost_box, 0, unroll=16)

    def couple(b, carry):
        total = None
        for kg in range(2):
            rows = []
            for k in range(8):
                source = ab[box_list[b, kg * 8 + k]]
                rows += [source * mlo, source * mhi]
            at = pl.ds(pl.multiple_of((b * 2 + kg) * 256, 256), 256)
            wide = dot_t(jnp.concatenate(rows, axis=0), coup[at, :])
            part = pick_slots([wide[s * 32 : s * 32 + 32] for s in range(8)])
            total = part if total is None else total + part
        fields[b] = total
        return carry

    lax.fori_loop(0, fields.shape[0], couple, 0, unroll=8)
    coupled = pltpu.make_async_copy(fields, fields_hbm, out_sems.at[1])
    coupled.start()

    first(0, 0)

    def items(i, carry):
        first(2 * i + 1, 1)
        second(2 * i, 0)
        first(2 * i + 2, 0)
        second(2 * i + 1, 1)
        return carry

    lax.fori_loop(0, rounds, items, 0)

    def join(v, carry):
        near_out[v] = jnp.concatenate([acc[2 * v], acc[2 * v + 1]], axis=1)
        return carry

    lax.fori_loop(0, half_tiles, join, 0, unroll=16)

    last = pltpu.make_async_copy(near_out, near_hbm, out_sems.at[0])
    last.start()
    coupled.wait()
    last.wait()


def fold(parts, unfold):
    rows = [jnp.concatenate([p[:16], p[16:]], axis=1) for p in parts]
    high = [r.astype(BF16) for r in rows]
    low = [(r - h.astype(F32)).astype(BF16) for r, h in zip(rows, high)]
    out = dot(jnp.concatenate(high + low, axis=0), unfold[...])
    n = 16 * len(parts)
    return out[:n] + out[n:]


def down_kernel(
    root_list,
    roots_in,
    rcoup_in,
    rtrans_in,
    fields_in,
    trans_in,
    basis_in,
    near_in,
    unfold_in,
    back_in,
    out_hbm,
    roots,
    rcoup,
    rtrans,
    fields,
    trans,
    basis,
    near,
    unfold,
    back,
    out,
    bf,
    far_high,
    far_low,
    sems,
    out_sems,
):
    def half_of(ref, rows):
        return ref.at[pl.ds(pl.multiple_of(lax.axis_index("sub") * rows, rows), rows)]

    pairs = [
        (roots_in, roots),
        (rcoup_in, rcoup),
        (unfold_in, unfold),
        (half_of(rtrans_in, rtrans.shape[0]), rtrans),
        (fields_in, fields),
    ]
    part = DOWN * 256
    parts = trans.shape[0] // part
    trans_half = half_of(trans_in, trans.shape[0])
    basis_half = half_of(basis_in, basis.shape[0])
    for i in range(parts):
        cut = pl.ds(i * part, part)
        pairs += [(trans_half.at[cut], trans.at[cut]), (basis_half.at[cut], basis.at[cut])]
    pairs += [(back_in, back), (near_in, near)]
    copies = copied(pairs, sems)
    for copy in copies[:3]:
        copy.wait()
    mlo, mhi = half_masks()
    low8 = low_half((8, 128))
    half_boxes = fields.shape[0]

    total = None
    known = rcoup.shape[0]
    for kg in range(2):
        rows = []
        have = min(known - kg * 8, 8)
        blocks = []
        for m in range(32):
            block = rcoup[:, m * 128 : m * 128 + 128].astype(F32)[kg * 8 : kg * 8 + have]
            if have < 8:
                block = jnp.concatenate([block, jnp.zeros((8 - have, 128), F32)], axis=0)
            blocks.append(block)
        matrix = jnp.concatenate(blocks, axis=0).astype(BF16)
        for k in range(8):
            if kg * 8 + k < known:
                source = roots[root_list[0, kg * 8 + k]].astype(F32)
                turned = roll_half(source)
                even = jnp.concatenate([source, turned], axis=0).astype(BF16) * mlo
                odd = jnp.concatenate([turned, source], axis=0).astype(BF16) * mhi
                rows += [even, odd]
            else:
                rows.append(jnp.zeros((32, 128), BF16))
        wide = dot_t(jnp.concatenate(rows, axis=0), matrix)
        part = pick_slots([wide[s * 32 : s * 32 + 32] for s in range(8)])
        total = part if total is None else total + part
    rf = fold([total], unfold).astype(BF16)
    moving = jnp.concatenate([rf * mlo, rf * mhi], axis=0)
    slot = lane_slot((32, 256))
    for copy in copies[3:5]:
        copy.wait()
    for g in range(half_boxes // 8):
        pushed = dot_t(moving, rtrans[g * 256 : g * 256 + 256, :])
        sums = [fields[g * 8 + s] + jnp.where(slot == s, pushed, 0.0) for s in range(8)]
        bf[g * 128 : g * 128 + 128, :] = fold(sums, unfold).astype(BF16)

    masks = slot_masks(16)

    def leaves(i):
        picks = [i * DOWN + j for j in range(DOWN)]
        rows = [pl.ds(pl.multiple_of(b * 256, 256), 256) for b in picks]
        spots = [pl.ds(pl.multiple_of(b * 16, 16), 16) for b in picks]
        hs = []
        for r, at in zip(rows, spots):
            field = bf[at, :]
            moving = jnp.concatenate([field * mlo, field * mhi], axis=0)
            hs.append(dot_t(moving, trans[r, :]).astype(BF16))
        wides = [
            jnp.concatenate(
                [jnp.concatenate([h[:16] * m, h[16:] * m], axis=1) for m in masks], axis=0
            )
            for h in hs
        ]
        lfs = [dot(wide, unfold[...]).astype(BF16) for wide in wides]
        fars = []
        for lf, r in zip(lfs, rows):
            parts = []
            for s in range(8):
                one = lf[s * 16 : s * 16 + 16]
                parts += [one * mlo, one * mhi]
            fars.append(dot_t(jnp.concatenate(parts, axis=0), basis[r, :]))
        for far, at in zip(fars, spots):
            far = pick_slots([far[s * 32 : s * 32 + 32] for s in range(8)])
            far = jnp.concatenate([far[:16], far[16:]], axis=1)
            high = far.astype(BF16)
            far_high[at, :] = high
            far_low[at, :] = (far - high.astype(F32)).astype(BF16)

    for i in range(parts):
        for copy in copies[5 + 2 * i : 7 + 2 * i]:
            copy.wait()
        leaves(i)

    for copy in copies[-2:]:
        copy.wait()

    def emit(i):
        at = pl.ds(i * 64, 64)
        far = dot(far_high[at, :], back[...]) + dot(far_low[at, :], back[...])
        for b in range(4):
            for j in range(4):
                v = (i * 4 + b) * 4 + j
                value = far[b * 16 : b * 16 + 16, j * 128 : j * 128 + 128] + near[v]
                out[:, pl.ds(v * 128, 128)] = value.astype(BF16)

    sends = []
    for i in range(half_boxes // 4):
        emit(i)
        cut = pl.ds(i * 2048, 2048)
        sends.append(pltpu.make_async_copy(out.at[:, cut], out_hbm.at[:, cut], out_sems.at[i]))
        sends[i].start()
    for send in sends:
        send.wait()


def natural(matrices):
    n = matrices.shape[0]
    return jnp.transpose(matrices.reshape(n // 8, 8, 32, 128), (0, 2, 1, 3)).reshape(n * 32, 128)


def whole(shape=None):
    return pl.BlockSpec(memory_space=VMEM)


def smem():
    return pl.BlockSpec(memory_space=pltpu.SMEM)


def shape_of(shape, dtype):
    return jax.ShapeDtypeStruct(shape, dtype)


def hbm():
    return pl.BlockSpec(memory_space=pltpu.HBM)


def params():
    return pltpu.CompilerParams(vmem_limit_bytes=66_900_000)


def swaps(peers, start):
    low = range(start, peers - 1, 2)
    return [(i, i + 1) for i in low] + [(i + 1, i) for i in low]


def per_device(
    density,
    coords,
    qweight,
    leaf_basis,
    box_transfer,
    root_transfer,
    box_coupling,
    root_coupling,
    near_list,
    near_count,
    box_list,
    root_list,
    ghost_send,
):
    points = density.shape[1]
    peers = lax.axis_size("leaf")
    tiles = points // 128
    box_count = tiles // 4
    half_leaves = near_list.shape[0]
    half_boxes = box_list.shape[0]
    basis = natural(leaf_basis)
    trans = natural(box_transfer)
    rtrans = natural(root_transfer)
    coup = natural(box_coupling.reshape(half_boxes * 16, 4096))
    rcoup = root_coupling[0]
    order = jnp.asarray(in_order_matrix(), BF16)
    back = jnp.asarray(in_order_matrix().T.copy(), BF16)
    spread_m = jnp.asarray(spread_matrix(), BF16)
    unfold = jnp.asarray(unfold_matrix(), BF16)

    zw, pay_one, pay_two, boxes, root = pl.pallas_call(
        up_kernel,
        name="up",
        out_shape=(
            shape_of((2 * tiles, 16, 128), BF16),
            shape_of((64, 16, 128), BF16),
            shape_of((64, 16, 128), BF16),
            shape_of((box_count, 16, 128), BF16),
            shape_of((peers, 8, 128), BF16),
        ),
        in_specs=[smem()] + [hbm()] * 8,
        out_specs=tuple([hbm()] * 5),
        scratch_shapes=[
            VMEM(density.shape, BF16),
            VMEM((1, points), F32),
            VMEM(coords.shape, F32),
            VMEM(basis.shape, BF16),
            VMEM(trans.shape, BF16),
            VMEM(rtrans.shape, BF16),
            VMEM(order.shape, BF16),
            VMEM(spread_m.shape, BF16),
            VMEM((box_count * 16, 512), BF16),
            VMEM((box_count * 16, 512), BF16),
            VMEM((2 * tiles, 8, 128), F32),
            VMEM((2 * tiles, 16, 128), BF16),
            VMEM((64, 16, 128), BF16),
            VMEM((64, 16, 128), BF16),
            VMEM((box_count, 16, 128), BF16),
            VMEM((peers, 8, 128), BF16),
            pltpu.SemaphoreType.DMA((6 + 2 * UP_PARTS,)),
            pltpu.SemaphoreType.DMA((5,)),
        ],
        compiler_params=params(),
    )(
        ghost_send,
        density,
        qweight.reshape(1, points),
        coords,
        basis,
        trans,
        rtrans,
        order,
        spread_m,
    )
    got_one = lax.ppermute(pay_one, "leaf", swaps(peers, 0))
    got_two = lax.ppermute(pay_two, "leaf", swaps(peers, 1))
    roots = lax.all_to_all(root, "leaf", 0, 0, tiled=True)

    table = 2 * (tiles + 64)
    near, fields = pl.pallas_call(
        near_kernel,
        name="near",
        out_shape=(
            shape_of((half_leaves // 2, 16, 128), F32),
            shape_of((half_boxes, 32, 256), F32),
        ),
        in_specs=[smem()] * 3 + [hbm()] * 6,
        out_specs=(hbm(), hbm()),
        scratch_shapes=[
            VMEM(coords.shape, F32),
            VMEM(got_one.shape, BF16),
            VMEM(got_two.shape, BF16),
            VMEM(coup.shape, BF16),
            VMEM((half_leaves // 2, 16, 128), F32),
            VMEM((half_boxes, 32, 256), F32),
            VMEM((table, 48, 128), BF16),
            VMEM((table, 16, 128), BF16),
            VMEM((half_leaves * 64, 48), BF16),
            VMEM((half_leaves + 1, 16, 64), F32),
            VMEM((3 * box_count, 16, 128), BF16),
            VMEM((2, ITEMS, 64, 256), BF16),
            VMEM((2, ITEMS, 16, 256), BF16),
            VMEM((52, 16, 128), BF16),
            pltpu.SMEM((half_leaves * 3 + 3 * ITEMS + 8,), jnp.int32),
            pltpu.SemaphoreType.DMA((6,)),
            pltpu.SemaphoreType.DMA((2,)),
        ],
        compiler_params=params(),
        cost_estimate=pl.CostEstimate(
            flops=4 * 10**10, bytes_accessed=10**7, transcendentals=6 * 10**6
        ),
    )(
        near_list.T,
        near_count,
        box_list,
        zw,
        coords,
        got_one,
        got_two,
        boxes,
        coup,
    )

    return pl.pallas_call(
        down_kernel,
        name="down",
        out_shape=shape_of((16, half_leaves * 64), BF16),
        in_specs=[smem()] + [hbm()] * 9,
        out_specs=hbm(),
        scratch_shapes=[
            VMEM(roots.shape, BF16),
            VMEM(rcoup.shape, BF16),
            VMEM((half_boxes * 32, 128), BF16),
            VMEM(fields.shape, F32),
            VMEM((half_leaves * 32, 128), BF16),
            VMEM((half_leaves * 32, 128), BF16),
            VMEM(near.shape, F32),
            VMEM(unfold.shape, BF16),
            VMEM(back.shape, BF16),
            VMEM((16, half_leaves * 64), BF16),
            VMEM((half_boxes * 16, 128), BF16),
            VMEM((half_boxes * 16, 512), BF16),
            VMEM((half_boxes * 16, 512), BF16),
            pltpu.SemaphoreType.DMA((7 + 2 * (half_boxes // DOWN),)),
            pltpu.SemaphoreType.DMA((half_boxes // 4,)),
        ],
        compiler_params=params(),
    )(root_list, roots, rcoup, rtrans, fields, trans, basis, near, unfold, back)


def solution(mesh):
    in_specs = (
        P(None, "leaf"),
        P(None, "leaf"),
        P("leaf"),
        P("leaf", None),
        P("leaf", None),
        P("leaf", None),
        P(("leaf", "sub"), None, None),
        P("leaf", None, None),
        P(("leaf", "sub"), None),
        P(("leaf", "sub")),
        P(("leaf", "sub"), None),
        P("leaf", None),
        P("leaf", "sub", None, None),
    )
    out_specs = P(None, ("leaf", "sub"))
    return jax.shard_map(
        per_device, mesh=mesh, in_specs=in_specs, out_specs=out_specs, check_vma=False
    )
```

```python
import functools

import jax
import jax.numpy as jnp
import numpy as np
from jax import lax
from jax.experimental import pallas as pl
from jax.experimental.pallas import tpu as pltpu
from jax.sharding import PartitionSpec as P

LEAF = 64
RANK = 64
DELTA_SQ = 0.0025
UP = 16
UP_PARTS = 4
ITEMS = 16
DOWN = 8
F32 = jnp.float32
BF16 = jnp.bfloat16
VMEM = pltpu.VMEM
NT = (((1,), (1,)), ((), ()))


def in_order_matrix():
    out = np.zeros((512, 512), np.float32)
    for leaf in range(8):
        for m in range(32):
            for par in range(2):
                out[leaf * 64 + 2 * m + par, par * 256 + m * 8 + leaf] = 1
    return out


def unfold_matrix():
    out = np.zeros((512, 128), np.float32)
    for par in range(2):
        for m in range(32):
            for leaf in range(8):
                out[par * 256 + m * 8 + leaf, 2 * m + par] = 1
                out[par * 256 + m * 8 + leaf, 64 + 2 * m + par] = 1
    return out


def spread_matrix():
    out = unfold_matrix().T.copy()
    out[64:] = 0
    return out


def dot(a, b):
    return jnp.dot(a, b, preferred_element_type=F32)


def dot_t(a, b):
    return lax.dot_general(a, b, NT, preferred_element_type=F32)


def low_half(shape):
    return lax.broadcasted_iota(jnp.int32, shape, len(shape) - 1) < 64


def lane_slot(shape):
    return lax.broadcasted_iota(jnp.int32, shape, len(shape) - 1) & 7


def roll_half(value):
    return pltpu.roll(value, 64, value.ndim - 1)


def half_masks():
    low = low_half((16, 128))
    return (
        jnp.where(low, 1.0, 0.0).astype(BF16),
        jnp.where(low, 0.0, 1.0).astype(BF16),
    )


def slot_masks(rows):
    slot = lane_slot((rows, 256))
    return [jnp.where(slot == s, 1.0, 0.0).astype(BF16) for s in range(8)]


def pick_slots(parts):
    slot = lane_slot(parts[0].shape)
    out = parts[0]
    for s in range(1, 8):
        out = jnp.where(slot == s, parts[s], out)
    return out


def add_halves(value):
    chosen = jnp.where(low_half((16, 128)), value[:16], value[16:])
    return chosen + roll_half(chosen)


def gathered(wide):
    picked = pick_slots([wide[s * 16 : s * 16 + 16] for s in range(8)]).astype(BF16)
    return jnp.concatenate([picked[:, :256], picked[:, 256:]], axis=0)


def copied(pairs, sems):
    copies = [pltpu.make_async_copy(a, b, sems.at[i]) for i, (a, b) in enumerate(pairs)]
    for copy in copies:
        copy.start()
    return copies


def up_kernel(
    send,
    dens_in,
    qw_in,
    coords_in,
    basis_in,
    trans_in,
    rtrans_in,
    order_in,
    spread_in,
    zw_out,
    pay_one_out,
    pay_two_out,
    boxes_out,
    root_out,
    dens,
    qw,
    coords,
    basis,
    trans,
    rtrans,
    order,
    spread_ref,
    flat,
    ordered,
    cz,
    rolled,
    pay_one,
    pay_two,
    boxes,
    root,
    sems,
    out_sems,
):
    part = basis.shape[0] // UP_PARTS
    pairs = [
        (dens_in, dens),
        (qw_in, qw),
        (coords_in, coords),
        (order_in, order),
        (spread_in, spread_ref),
    ]
    for i in range(UP_PARTS):
        cut = pl.ds(i * part, part)
        pairs += [(basis_in.at[cut], basis.at[cut]), (trans_in.at[cut], trans.at[cut])]
    pairs.append((rtrans_in, rtrans))
    copies = copied(pairs, sems)
    for copy in copies[:3]:
        copy.wait()
    tiles = dens.shape[1] // 128
    box_count = tiles // 4
    mlo, mhi = half_masks()

    def weigh(b, carry):
        at = pl.multiple_of(b * 512, 512)
        row = pl.multiple_of(b * 16, 16)
        w = (dens[:, pl.ds(at, 512)].astype(F32) * qw[:, pl.ds(at, 512)]).astype(BF16)
        flat[pl.ds(row, 16), :] = w
        wide = w.astype(F32)
        c = coords[:, pl.ds(at, 512)]
        c = jnp.concatenate([c, jnp.zeros((5, 512), F32)], axis=0)
        for j in range(4):
            v = b * 4 + j
            cut = slice(j * 128, j * 128 + 128)
            rolled[2 * v] = w[:, cut]
            rolled[2 * v + 1] = roll_half(wide[:, cut]).astype(BF16)
            cz[2 * v] = c[:, cut]
            cz[2 * v + 1] = roll_half(c[:, cut])
        return carry

    lax.fori_loop(0, box_count, weigh, 0, unroll=8)

    kept = pltpu.make_async_copy(rolled, zw_out, out_sems.at[0])
    copies[3].wait()
    ordered[...] = dot(flat[...], order[...]).astype(BF16)

    low8 = low_half((8, 128))
    odd = lax.axis_index("leaf") & 1

    def pack(i, carry):
        for d, pay in ((odd, pay_one), (1 - odd, pay_two)):
            parts = []
            for j in range(2):
                pair = i * 2 + j
                s0 = send[0, 0, d, pair * 2]
                s1 = send[0, 0, d, pair * 2 + 1]
                i0 = s0
                i1 = s1 ^ 1
                pay[pair] = rolled[i0] * mlo + rolled[i1] * mhi
                c = jnp.where(low8, cz[i0], cz[i1])
                high = c.astype(BF16).astype(F32)
                parts += [high[0:4], (c - high)[0:4]]
            pay[32 + i] = jnp.concatenate(parts, axis=0).astype(BF16)
        return carry

    lax.fori_loop(0, 16, pack, 0, unroll=8)

    masks = slot_masks(32)

    copies[4].wait()

    def up(i):
        picks = [i * UP + j for j in range(UP)]
        rows = [pl.ds(pl.multiple_of(b * 256, 256), 256) for b in picks]
        outs = []
        for b, r in zip(picks, rows):
            w = ordered[pl.ds(pl.multiple_of(b * 16, 16), 16), :]
            w = jnp.concatenate([w[:, :256], w[:, 256:]], axis=0)
            moving = jnp.concatenate([w * m for m in masks], axis=0)
            outs.append(dot(moving, basis[r, :]))
        coefs = [
            jnp.concatenate(
                [add_halves(out[s * 32 : s * 32 + 32]) for s in range(8)], axis=0
            ).astype(BF16)
            for out in outs
        ]
        wides = [dot(c, spread_ref[...]) for c in coefs]
        lifted = [dot(gathered(w), trans[r, :]) for w, r in zip(wides, rows)]
        for b, total in zip(picks, lifted):
            boxes[b] = add_halves(total).astype(BF16)

    steps = box_count // UP
    waits = 2 * UP_PARTS // steps
    for i in range(steps):
        for copy in copies[5 + i * waits : 5 + i * waits + waits]:
            copy.wait()
        up(i)
        if i == 0:
            kept.start()

    def finish(i, carry):
        pair = boxes[2 * i] * mlo + boxes[2 * i + 1] * mhi
        pay_one[48 + i] = pair
        pay_two[48 + i] = pair
        return carry

    lax.fori_loop(0, box_count // 2, finish, 0, unroll=4)

    sends = [
        pltpu.make_async_copy(a, b, out_sems.at[i])
        for i, (a, b) in ((1, (pay_one, pay_one_out)), (2, (pay_two, pay_two_out)), (3, (boxes, boxes_out)))
    ]
    for copy in sends:
        copy.start()
    copies[-1].wait()
    wides = [
        dot(jnp.concatenate([boxes[g * 8 + s] for s in range(8)], axis=0), spread_ref[...])
        for g in range(box_count // 8)
    ]
    total = jnp.zeros((32, 128), F32)
    for g, wide in enumerate(wides):
        total += dot(gathered(wide), rtrans[g * 256 : g * 256 + 256, :])
    total = add_halves(total)
    total = jnp.where(low8, total[:8], total[8:]).astype(BF16)

    def copy_root(i, carry):
        root[i] = total
        return carry

    lax.fori_loop(0, root.shape[0], copy_root, 0, unroll=16)
    last = pltpu.make_async_copy(root, root_out, out_sems.at[4])
    last.start()
    for copy in sends + [kept, last]:
        copy.wait()


def split3(value):
    high = value.astype(BF16).astype(F32)
    rest = value - high
    mid = rest.astype(BF16).astype(F32)
    return high, mid, rest - mid


def near_kernel(
    near,
    count,
    box_list,
    zw,
    coords_in,
    got_one,
    got_two,
    boxes,
    coup_in,
    near_hbm,
    fields_hbm,
    coords,
    extra_one,
    extra_two,
    coup,
    near_out,
    fields,
    feats,
    wz,
    tt,
    acc,
    ab,
    kernels,
    weights,
    live_masks,
    slots,
    sems,
    out_sems,
):
    half_leaves = count.shape[0]
    own_tiles = zw.shape[0] // 2
    ghost = 32
    half_tiles = own_tiles // 2
    mlo, mhi = half_masks()
    own_boxes = boxes.shape[0]
    copies = copied(
        (
            (coords_in, coords),
            (zw, wz.at[pl.ds(0, 2 * own_tiles)]),
            (got_one, extra_one),
            (got_two, extra_two),
            (boxes, ab.at[pl.ds(0, own_boxes)]),
            (coup_in, coup),
        ),
        sems,
    )

    def listing(t, listed):
        for k in range(3):
            slots[listed + k] = t * 516 + k
        return listed + ((count[t] + 3) >> 2)

    listed = lax.fori_loop(0, half_leaves, listing, 0, unroll=8)
    for k in range(3 * ITEMS):
        slots[listed + k] = half_leaves * 512
    rounds = (listed + 2 * ITEMS - 1) // (2 * ITEMS)

    def clear(i, carry):
        acc[i] = jnp.zeros((16, 64), F32)
        return carry

    lax.fori_loop(0, 2 * half_tiles + 1, clear, 0, unroll=8)

    for n in range(13):
        for k in range(4):
            part = (mlo, mhi)[k % 2]
            live_masks[n * 4 + k] = part if k < n else jnp.zeros_like(part)

    def source_pair(e0, e1):
        one = feats[e0]
        two = feats[e1 ^ 1]
        return jnp.concatenate(
            [one[r : r + 16] * mlo + two[r : r + 16] * mhi for r in range(0, 48, 16)], axis=0
        )

    def weight_pair(e0, e1, at):
        return wz[e0] * live_masks[at] + wz[e1 ^ 1] * live_masks[at + 1]

    def first(group, buffer):
        squares = []
        for j in range(ITEMS):
            v = slots[group * ITEMS + j]
            t = (v >> 2) & (half_leaves - 1)
            at = (v & 3) * 4
            live = (count[t] - at) * 4
            e = [near[at + k, t] for k in range(4)]
            source = jnp.concatenate([source_pair(e[0], e[1]), source_pair(e[2], e[3])], axis=1)
            weights[buffer, j] = jnp.concatenate(
                [weight_pair(e[0], e[1], live), weight_pair(e[2], e[3], live + 2)], axis=1
            )
            squares.append(dot(tt[pl.ds(pl.multiple_of(t * 64, 64), 64), :], source))
        for j, square in enumerate(squares):
            kernels[buffer, j] = lax.rsqrt(square).astype(BF16)

    def second(group, buffer):
        values = [dot_t(weights[buffer, j], kernels[buffer, j]) for j in range(ITEMS)]
        for j, value in enumerate(values):
            acc[slots[group * ITEMS + j] >> 9] += value

    copies[0].wait()
    row8 = lax.broadcasted_iota(jnp.int32, (8, 128), 0)

    def put_source(v, c):
        c = jnp.where(row8 < 3, c - 0.5, 0.0)
        size = jnp.sum(c * c, axis=0, keepdims=True)
        u = jnp.where(row8 < 3, c, jnp.where(row8 == 3, size, jnp.where(row8 == 4, 1.0, 0.0)))
        for at, block in ((2 * v, u), (2 * v + 1, roll_half(u))):
            h, m, l = split3(block)
            feats[at] = jnp.concatenate([h, m, l, h, m, h], axis=0).astype(BF16)

    def own(i, carry):
        for j in range(32):
            v = i * 32 + j
            c = coords[:, pl.ds(pl.multiple_of(v * 128, 128), 128)]
            c = jnp.concatenate([c, jnp.zeros((5, 128), F32)], axis=0)
            put_source(v, c)
        return carry

    lax.fori_loop(0, own_tiles // 32, own, 0)
    eye = jnp.where(
        lax.broadcasted_iota(jnp.int32, (128, 128), 0)
        == lax.broadcasted_iota(jnp.int32, (128, 128), 1),
        1.0,
        0.0,
    ).astype(BF16)
    first_tile = lax.axis_index("sub") * half_tiles

    def target(i, carry):
        blocks = []
        for j in range(32):
            v = i * 32 + j
            c = coords[:, pl.ds(pl.multiple_of((first_tile + v) * 128, 128), 128)]
            c = jnp.concatenate([c, jnp.zeros((5, 128), F32)], axis=0)
            c = jnp.where(row8 < 3, c - 0.5, 0.0)
            size = jnp.sum(c * c, axis=0, keepdims=True) + DELTA_SQ
            u = jnp.where(
                row8 < 3, -2.0 * c, jnp.where(row8 == 3, 1.0, jnp.where(row8 == 4, size, 0.0))
            )
            h, m, l = split3(u)
            blocks.append(jnp.concatenate([h, h, h, m, m, l], axis=0).astype(BF16))
        for j, turned in enumerate([dot_t(eye, block) for block in blocks]):
            tt[pl.ds(pl.multiple_of((i * 32 + j) * 128, 128), 128), :] = turned.astype(BF16)
        return carry

    lax.fori_loop(0, half_tiles // 32, target, 0)

    for copy in copies[1:4]:
        copy.wait()
    odd = lax.axis_index("leaf") & 1
    for base, pay in (
        (own_tiles + ghost * (1 - odd), extra_one),
        (own_tiles + ghost * odd, extra_two),
    ):

        def ghosts(i, carry, base=base, pay=pay):
            both = pay[32 + i].astype(F32)
            for j in range(2):
                v = i * 2 + j
                c = both[j * 8 : j * 8 + 4] + both[j * 8 + 4 : j * 8 + 8]
                c = jnp.concatenate([c, jnp.zeros((4, 128), F32)], axis=0)
                put_source(base + v, c)
                wz[2 * (base + v)] = pay[v]
                wz[2 * (base + v) + 1] = roll_half(pay[v].astype(F32)).astype(BF16)
            return carry

        lax.fori_loop(0, ghost // 2, ghosts, 0, unroll=16)

    for copy in copies[4:]:
        copy.wait()
    low16 = low_half((16, 128))
    for base, pay in (
        (own_boxes * (2 - odd), extra_one),
        (own_boxes * (1 + odd), extra_two),
    ):

        def ghost_box(i, carry, base=base, pay=pay):
            pair = pay[48 + i].astype(F32)
            turned = roll_half(pair)
            ab[base + 2 * i] = jnp.where(low16, pair, turned).astype(BF16)
            ab[base + 2 * i + 1] = jnp.where(low16, turned, pair).astype(BF16)
            return carry

        lax.fori_loop(0, own_boxes // 2, ghost_box, 0, unroll=16)

    def couple(b, carry):
        total = None
        for kg in range(2):
            rows = []
            for k in range(8):
                source = ab[box_list[b, kg * 8 + k]]
                rows += [source * mlo, source * mhi]
            at = pl.ds(pl.multiple_of((b * 2 + kg) * 256, 256), 256)
            wide = dot_t(jnp.concatenate(rows, axis=0), coup[at, :])
            part = pick_slots([wide[s * 32 : s * 32 + 32] for s in range(8)])
            total = part if total is None else total + part
        fields[b] = total
        return carry

    lax.fori_loop(0, fields.shape[0], couple, 0, unroll=8)
    coupled = pltpu.make_async_copy(fields, fields_hbm, out_sems.at[4])
    coupled.start()

    first(0, 0)

    def items(i, carry):
        first(2 * i + 1, 1)
        second(2 * i, 0)
        first(2 * i + 2, 0)
        second(2 * i + 1, 1)
        return carry

    lax.fori_loop(0, rounds, items, 0)

    def join(v, carry):
        near_out[v] = jnp.concatenate([acc[2 * v], acc[2 * v + 1]], axis=1)
        return carry

    sends = []
    for i in range(4):
        lax.fori_loop(i * (half_tiles // 4), (i + 1) * (half_tiles // 4), join, 0, unroll=16)
        cut = pl.ds(i * (half_tiles // 4), half_tiles // 4)
        sends.append(pltpu.make_async_copy(near_out.at[cut], near_hbm.at[cut], out_sems.at[i]))
        sends[i].start()

    coupled.wait()
    for send in sends:
        send.wait()


def fold(parts, unfold):
    rows = [jnp.concatenate([p[:16], p[16:]], axis=1) for p in parts]
    high = [r.astype(BF16) for r in rows]
    low = [(r - h.astype(F32)).astype(BF16) for r, h in zip(rows, high)]
    out = dot(jnp.concatenate(high + low, axis=0), unfold[...])
    n = 16 * len(parts)
    return out[:n] + out[n:]


def down_kernel(
    root_list,
    roots_in,
    rcoup_in,
    rtrans_in,
    fields_in,
    trans_in,
    basis_in,
    near_in,
    unfold_in,
    back_in,
    out_hbm,
    roots,
    rcoup,
    rtrans,
    fields,
    trans,
    basis,
    near,
    unfold,
    back,
    out,
    bf,
    far_high,
    far_low,
    sems,
    out_sems,
):
    def half_of(ref, rows):
        return ref.at[pl.ds(pl.multiple_of(lax.axis_index("sub") * rows, rows), rows)]

    pairs = [
        (roots_in, roots),
        (rcoup_in, rcoup),
        (unfold_in, unfold),
        (half_of(rtrans_in, rtrans.shape[0]), rtrans),
        (fields_in, fields),
    ]
    part = DOWN * 256
    parts = trans.shape[0] // part
    trans_half = half_of(trans_in, trans.shape[0])
    basis_half = half_of(basis_in, basis.shape[0])
    for i in range(parts):
        cut = pl.ds(i * part, part)
        pairs += [(trans_half.at[cut], trans.at[cut]), (basis_half.at[cut], basis.at[cut])]
    pairs += [(back_in, back), (near_in, near)]
    copies = copied(pairs, sems)
    for copy in copies[:3]:
        copy.wait()
    mlo, mhi = half_masks()
    low8 = low_half((8, 128))
    half_boxes = fields.shape[0]

    total = None
    known = rcoup.shape[0]
    for kg in range(2):
        rows = []
        have = min(known - kg * 8, 8)
        blocks = []
        for m in range(32):
            block = rcoup[:, m * 128 : m * 128 + 128].astype(F32)[kg * 8 : kg * 8 + have]
            if have < 8:
                block = jnp.concatenate([block, jnp.zeros((8 - have, 128), F32)], axis=0)
            blocks.append(block)
        matrix = jnp.concatenate(blocks, axis=0).astype(BF16)
        for k in range(8):
            if kg * 8 + k < known:
                source = roots[root_list[0, kg * 8 + k]].astype(F32)
                turned = roll_half(source)
                even = jnp.concatenate([source, turned], axis=0).astype(BF16) * mlo
                odd = jnp.concatenate([turned, source], axis=0).astype(BF16) * mhi
                rows += [even, odd]
            else:
                rows.append(jnp.zeros((32, 128), BF16))
        wide = dot_t(jnp.concatenate(rows, axis=0), matrix)
        part = pick_slots([wide[s * 32 : s * 32 + 32] for s in range(8)])
        total = part if total is None else total + part
    rf = fold([total], unfold).astype(BF16)
    moving = jnp.concatenate([rf * mlo, rf * mhi], axis=0)
    slot = lane_slot((32, 256))
    for copy in copies[3:5]:
        copy.wait()
    for g in range(half_boxes // 8):
        pushed = dot_t(moving, rtrans[g * 256 : g * 256 + 256, :])
        sums = [fields[g * 8 + s] + jnp.where(slot == s, pushed, 0.0) for s in range(8)]
        bf[g * 128 : g * 128 + 128, :] = fold(sums, unfold).astype(BF16)

    masks = slot_masks(16)

    def leaves(i):
        picks = [i * DOWN + j for j in range(DOWN)]
        rows = [pl.ds(pl.multiple_of(b * 256, 256), 256) for b in picks]
        spots = [pl.ds(pl.multiple_of(b * 16, 16), 16) for b in picks]
        hs = []
        for r, at in zip(rows, spots):
            field = bf[at, :]
            moving = jnp.concatenate([field * mlo, field * mhi], axis=0)
            hs.append(dot_t(moving, trans[r, :]).astype(BF16))
        wides = [
            jnp.concatenate(
                [jnp.concatenate([h[:16] * m, h[16:] * m], axis=1) for m in masks], axis=0
            )
            for h in hs
        ]
        lfs = [dot(wide, unfold[...]).astype(BF16) for wide in wides]
        fars = []
        for lf, r in zip(lfs, rows):
            parts = []
            for s in range(8):
                one = lf[s * 16 : s * 16 + 16]
                parts += [one * mlo, one * mhi]
            fars.append(dot_t(jnp.concatenate(parts, axis=0), basis[r, :]))
        for far, at in zip(fars, spots):
            far = pick_slots([far[s * 32 : s * 32 + 32] for s in range(8)])
            far = jnp.concatenate([far[:16], far[16:]], axis=1)
            high = far.astype(BF16)
            far_high[at, :] = high
            far_low[at, :] = (far - high.astype(F32)).astype(BF16)

    for i in range(parts):
        for copy in copies[5 + 2 * i : 7 + 2 * i]:
            copy.wait()
        leaves(i)

    for copy in copies[-2:]:
        copy.wait()

    def emit(i):
        at = pl.ds(i * 64, 64)
        far = dot(far_high[at, :], back[...]) + dot(far_low[at, :], back[...])
        for b in range(4):
            for j in range(4):
                v = (i * 4 + b) * 4 + j
                value = far[b * 16 : b * 16 + 16, j * 128 : j * 128 + 128] + near[v]
                out[:, pl.ds(v * 128, 128)] = value.astype(BF16)

    sends = []
    for i in range(half_boxes // 4):
        emit(i)
        cut = pl.ds(i * 2048, 2048)
        sends.append(pltpu.make_async_copy(out.at[:, cut], out_hbm.at[:, cut], out_sems.at[i]))
        sends[i].start()
    for send in sends:
        send.wait()


def natural(matrices):
    n = matrices.shape[0]
    return jnp.transpose(matrices.reshape(n // 8, 8, 32, 128), (0, 2, 1, 3)).reshape(n * 32, 128)


def whole(shape=None):
    return pl.BlockSpec(memory_space=VMEM)


def smem():
    return pl.BlockSpec(memory_space=pltpu.SMEM)


def shape_of(shape, dtype):
    return jax.ShapeDtypeStruct(shape, dtype)


def hbm():
    return pl.BlockSpec(memory_space=pltpu.HBM)


def params():
    return pltpu.CompilerParams(vmem_limit_bytes=66_900_000)


def swaps(peers, start):
    low = range(start, peers - 1, 2)
    return [(i, i + 1) for i in low] + [(i + 1, i) for i in low]


def per_device(
    density,
    coords,
    qweight,
    leaf_basis,
    box_transfer,
    root_transfer,
    box_coupling,
    root_coupling,
    near_list,
    near_count,
    box_list,
    root_list,
    ghost_send,
):
    points = density.shape[1]
    peers = lax.axis_size("leaf")
    tiles = points // 128
    box_count = tiles // 4
    half_leaves = near_list.shape[0]
    half_boxes = box_list.shape[0]
    basis = natural(leaf_basis)
    trans = natural(box_transfer)
    rtrans = natural(root_transfer)
    coup = natural(box_coupling.reshape(half_boxes * 16, 4096))
    rcoup = root_coupling[0]
    order = jnp.asarray(in_order_matrix(), BF16)
    back = jnp.asarray(in_order_matrix().T.copy(), BF16)
    spread_m = jnp.asarray(spread_matrix(), BF16)
    unfold = jnp.asarray(unfold_matrix(), BF16)

    zw, pay_one, pay_two, boxes, root = pl.pallas_call(
        up_kernel,
        name="up",
        out_shape=(
            shape_of((2 * tiles, 16, 128), BF16),
            shape_of((64, 16, 128), BF16),
            shape_of((64, 16, 128), BF16),
            shape_of((box_count, 16, 128), BF16),
            shape_of((peers, 8, 128), BF16),
        ),
        in_specs=[smem()] + [hbm()] * 8,
        out_specs=tuple([hbm()] * 5),
        scratch_shapes=[
            VMEM(density.shape, BF16),
            VMEM((1, points), F32),
            VMEM(coords.shape, F32),
            VMEM(basis.shape, BF16),
            VMEM(trans.shape, BF16),
            VMEM(rtrans.shape, BF16),
            VMEM(order.shape, BF16),
            VMEM(spread_m.shape, BF16),
            VMEM((box_count * 16, 512), BF16),
            VMEM((box_count * 16, 512), BF16),
            VMEM((2 * tiles, 8, 128), F32),
            VMEM((2 * tiles, 16, 128), BF16),
            VMEM((64, 16, 128), BF16),
            VMEM((64, 16, 128), BF16),
            VMEM((box_count, 16, 128), BF16),
            VMEM((peers, 8, 128), BF16),
            pltpu.SemaphoreType.DMA((6 + 2 * UP_PARTS,)),
            pltpu.SemaphoreType.DMA((5,)),
        ],
        compiler_params=params(),
    )(
        ghost_send,
        density,
        qweight.reshape(1, points),
        coords,
        basis,
        trans,
        rtrans,
        order,
        spread_m,
    )
    got_one = lax.ppermute(pay_one, "leaf", swaps(peers, 0))
    got_two = lax.ppermute(pay_two, "leaf", swaps(peers, 1))
    roots = lax.all_to_all(root, "leaf", 0, 0, tiled=True)

    table = 2 * (tiles + 64)
    near, fields = pl.pallas_call(
        near_kernel,
        name="near",
        out_shape=(
            shape_of((half_leaves // 2, 16, 128), F32),
            shape_of((half_boxes, 32, 256), F32),
        ),
        in_specs=[smem()] * 3 + [hbm()] * 6,
        out_specs=(hbm(), hbm()),
        scratch_shapes=[
            VMEM(coords.shape, F32),
            VMEM(got_one.shape, BF16),
            VMEM(got_two.shape, BF16),
            VMEM(coup.shape, BF16),
            VMEM((half_leaves // 2, 16, 128), F32),
            VMEM((half_boxes, 32, 256), F32),
            VMEM((table, 48, 128), BF16),
            VMEM((table, 16, 128), BF16),
            VMEM((half_leaves * 64, 48), BF16),
            VMEM((half_leaves + 1, 16, 64), F32),
            VMEM((3 * box_count, 16, 128), BF16),
            VMEM((2, ITEMS, 64, 256), BF16),
            VMEM((2, ITEMS, 16, 256), BF16),
            VMEM((52, 16, 128), BF16),
            pltpu.SMEM((half_leaves * 3 + 3 * ITEMS + 8,), jnp.int32),
            pltpu.SemaphoreType.DMA((6,)),
            pltpu.SemaphoreType.DMA((5,)),
        ],
        compiler_params=params(),
        cost_estimate=pl.CostEstimate(
            flops=4 * 10**10, bytes_accessed=10**7, transcendentals=6 * 10**6
        ),
    )(
        near_list.T,
        near_count,
        box_list,
        zw,
        coords,
        got_one,
        got_two,
        boxes,
        coup,
    )

    return pl.pallas_call(
        down_kernel,
        name="down",
        out_shape=shape_of((16, half_leaves * 64), BF16),
        in_specs=[smem()] + [hbm()] * 9,
        out_specs=hbm(),
        scratch_shapes=[
            VMEM(roots.shape, BF16),
            VMEM(rcoup.shape, BF16),
            VMEM((half_boxes * 32, 128), BF16),
            VMEM(fields.shape, F32),
            VMEM((half_leaves * 32, 128), BF16),
            VMEM((half_leaves * 32, 128), BF16),
            VMEM(near.shape, F32),
            VMEM(unfold.shape, BF16),
            VMEM(back.shape, BF16),
            VMEM((16, half_leaves * 64), BF16),
            VMEM((half_boxes * 16, 128), BF16),
            VMEM((half_boxes * 16, 512), BF16),
            VMEM((half_boxes * 16, 512), BF16),
            pltpu.SemaphoreType.DMA((7 + 2 * (half_boxes // DOWN),)),
            pltpu.SemaphoreType.DMA((half_boxes // 4,)),
        ],
        compiler_params=params(),
    )(root_list, roots, rcoup, rtrans, fields, trans, basis, near, unfold, back)


def solution(mesh):
    in_specs = (
        P(None, "leaf"),
        P(None, "leaf"),
        P("leaf"),
        P("leaf", None),
        P("leaf", None),
        P("leaf", None),
        P(("leaf", "sub"), None, None),
        P("leaf", None, None),
        P(("leaf", "sub"), None),
        P(("leaf", "sub")),
        P(("leaf", "sub"), None),
        P("leaf", None),
        P("leaf", "sub", None, None),
    )
    out_specs = P(None, ("leaf", "sub"))
    return jax.shard_map(
        per_device, mesh=mesh, in_specs=in_specs, out_specs=out_specs, check_vma=False
    )
```
